256 devices in a mesh: dp: 2 (over core), ctx: 4 (over x), head: 32 (over z, y).
Axes of the slice: x: 4, y: 4, z: 8, core: 2. Of those that a mesh axis runs over, the one named last changes fastest.
Arguments:
- query: bfloat16 [2, 2048, 24576], P('dp', 'ctx', 'head'), may hold values from -240 to 240
- kv_latent: bfloat16 [2, 2048, 576], P('dp', ('ctx', 'head')), may hold values from -4 to 4
- kv_weight: bfloat16 [512, 32768], P(None, 'head'), may hold values from -0.25 to 0.25
- grad_out: bfloat16 [2, 2048, 16384], P('dp', 'ctx', 'head'), may hold values from -6 to 6
- doc_lengths: int32 [2, 16], P('dp'), may hold values from 1 to 512, 2048 in all within a row
Outputs:
- d_query: bfloat16 [2, 2048, 24576], P('dp', 'ctx', 'head')
- d_latent: bfloat16 [2, 2048, 576], P('dp', ('ctx', 'head'))
- d_kv_weight: float32 [512, 32768], P(None, 'head')
The draws below stay inside these ranges and needn't reach their ends.
Inputs may be any that keep to these rules, and one draw needn't show every extreme that they name: `doc_lengths`: each row sums to 2048 and holds one length of exactly 512.
All inputs are finite; a program needn't handle non-finite values.
Results may differ from the reference program's by a relative error of at most 0.014.
Values may be sent and summed in bfloat16 or wider, within the bound.
No kernel may reach another device: no remote copies, remote signals or barrier semaphores. Data moves between devices by JAX's collectives and lax.ppermute only.
A program may use at most 128 MiB of HBM per device.

```python
import math
import jax
import jax.numpy as jnp
import numpy as np
from jax import lax

LATENT = 512
ROPE = 64
NOPE = 128
VDIM = 128
HEADS = 128
TOK_CTX = 512
DOC_MAX = 512
BLOCK = 512
TOKENS = 2048
REPLICAS = 2
DOCS = 16
N_CTX = 4


def rope_rows(key):
    rotary = jax.random.normal(jax.random.fold_in(key, 11), (REPLICAS, TOKENS, ROPE), jnp.float32)
    rotary = jnp.clip(rotary, -4.0, 4.0)
    return rotary


def draw_kv_latent(key, part):
    rotary = rope_rows(key)
    key = jax.random.fold_in(key, 1)
    latent = jnp.clip(jax.random.normal(key, (REPLICAS, TOKENS, LATENT), jnp.float32), -4.0, 4.0)
    return jnp.concatenate([latent, rotary], axis=-1).astype(jnp.bfloat16)


def draw_query(key, part):
    key = jax.random.fold_in(key, 2)
    shape = (REPLICAS, TOKENS, HEADS, NOPE + ROPE)
    base = jnp.clip(jax.random.normal(key, shape, jnp.float32), -4.0, 4.0)
    return base.reshape(REPLICAS, TOKENS, HEADS * (NOPE + ROPE)).astype(jnp.bfloat16)


def with_spikes(values, rng, source, target, blocks, factor):
    owner, partner = [(jnp.arange(values.shape[axis_at]) // (values.shape[axis_at] // blocks)).reshape([-1 if axis == axis_at else 1 for axis in range(values.ndim)]) for axis_at in (source, target)]
    chosen = jax.random.permutation(rng, blocks)[partner]
    strong = (owner == chosen) | (owner == (partner + blocks // 2) % blocks)
    return jnp.where(strong, factor * values, values)


def levels(stream_key, dims, split, least, top_value):
    gain = 1.0
    for dim, shards_of in split:
        draws = jax.random.uniform(jax.random.fold_in(jax.random.fold_in(stream_key, 6), dim), (shards_of,), jnp.float32, least / len(split), top_value / len(split))
        gain = gain * jnp.repeat(jnp.exp(draws), dims[dim] // shards_of).reshape((-1,) + (1,) * (len(dims) - 1 - dim))
    return gain


def split_up(amount, total, reach, skew):
    weights = [(1 << 20) // math.isqrt(grade ** skew) + 1 for grade in range(2, amount + 1)]
    rest, counts = total - reach - (amount - 1), [1] * (amount - 1)
    while rest > 0:
        candidates = [i for i in range(amount - 1) if counts[i] < reach]
        pool, left = sum([weights[i] for i in candidates]), rest
        for i in candidates:
            addition = min(reach - counts[i], max(1, left * weights[i] // pool), rest)
            counts[i] = counts[i] + addition
            rest = rest - addition
    return np.array([reach] + counts)


def ragged_sizes(key, count, total, bound, lean):
    if count == 2:
        one = jax.random.randint(key, (), max(1, total - bound), min(bound, total - 1) + 1)
        return jnp.stack([one, total - one])
    sizes = jnp.asarray(split_up(count, total, bound, lean), jnp.int32)
    pairs = (count - 1) // 2
    source_of, sink = sizes[1:1 + 2 * pairs:2], sizes[2:2 + 2 * pairs:2]
    margin = jnp.minimum(source_of - 1, bound - sink)
    shifted = jax.random.randint(jax.random.fold_in(key, 1), (pairs,), 0, 1 << 20) % (margin + 1)
    sizes = sizes.at[1:1 + 2 * pairs:2].set(source_of - shifted).at[2:2 + 2 * pairs:2].set(sink + shifted)
    return sizes[jax.random.permutation(jax.random.fold_in(key, 2), count)]


def gaussian(rng, extent, scale, bound, cuts=(), kind=jnp.bfloat16):
    result = jax.random.normal(rng, extent, jnp.float32) * scale
    if len(cuts) > 0:
        result = levels(rng, extent, cuts, -0.22, 0.18) * result
    return jnp.clip(result, min=-bound, max=bound).astype(kind)


def heavy_noise(stream_key, extent, width, reach, cuts, heavy, held_as=jnp.bfloat16):
    entries = width * jax.random.normal(stream_key, extent, jnp.float32)
    if cuts:
        entries = entries * levels(stream_key, extent, cuts, -0.22, 0.18)
    return jnp.clip(with_spikes(entries, jax.random.fold_in(stream_key, 3), *heavy), -reach, reach).astype(held_as)


def setup_inputs(seed: int = 0) -> dict:
    key_of = jax.random.split(jax.random.key(seed), 6)
    return {
        "query": draw_query(jax.random.fold_in(key_of[5], 71), 0),
        "kv_latent": draw_kv_latent(jax.random.fold_in(key_of[5], 71), 0),
        "kv_weight": gaussian(key_of[2], (LATENT, HEADS * (NOPE + VDIM)), LATENT ** -0.5, 0.25, ((1, 32),)),
        "grad_out": heavy_noise(key_of[3], (REPLICAS, TOKENS, HEADS * VDIM), 1.0, 6.0, ((0, 2), (1, 4), (2, 32)), (2, 1, 32, 2.75)),
        "doc_lengths": jax.vmap(lambda own: ragged_sizes(own, DOCS, TOKENS, DOC_MAX, 2))(jax.random.split(key_of[4], REPLICAS)).reshape((REPLICAS, DOCS)).astype(jnp.int32),
    }


def attend(query_block, grad_block, key_nope, key_rope, value_rows, query_doc, key_doc, query_pos, key_pos, factor):
    query_f = query_block.astype(jnp.float32)
    grad_f = grad_block.astype(jnp.float32)
    query_nope = query_f[..., :NOPE]
    query_rope = query_f[..., NOPE:]
    knope_f = key_nope.astype(jnp.float32)
    krope_f = key_rope.astype(jnp.float32)
    value_f = value_rows.astype(jnp.float32)
    scores = (jnp.einsum("qhd,khd->hqk", query_nope, knope_f) + jnp.einsum("qhd,kd->hqk", query_rope, krope_f)) * factor
    allowed = (query_doc[:, None] == key_doc[None, :]) & (key_pos[None, :] <= query_pos[:, None])
    scores = jnp.where(allowed[None], scores, -1e30)
    top_score = jnp.max(scores, axis=-1, keepdims=True)
    weights = jnp.where(allowed[None], jnp.exp(scores - top_score), 0.0)
    prob = weights / jnp.sum(weights, axis=-1, keepdims=True)
    prob_low = lax.optimization_barrier(prob.astype(jnp.bfloat16)).astype(jnp.float32)
    output = jnp.einsum("hqk,khd->qhd", prob_low, value_f)
    delta = jnp.sum(grad_f * output, axis=-1)
    dots = jnp.einsum("qhd,khd->hqk", grad_f, value_f)
    slope = lax.optimization_barrier((prob * (dots - delta.T[:, :, None])).astype(jnp.bfloat16)).astype(jnp.float32)
    grad_nope = jnp.einsum("hqk,khd->qhd", slope, knope_f) * factor
    grad_rot = jnp.einsum("hqk,kd->qhd", slope, krope_f) * factor
    grad_query = jnp.concatenate([grad_nope, grad_rot], axis=-1).astype(jnp.bfloat16)
    grad_key = jnp.einsum("hqk,qhd->khd", slope, query_nope) * factor
    grad_value = jnp.einsum("hqk,qhd->khd", prob_low, grad_f)
    grad_rope = jnp.einsum("hqk,qhd->kd", slope, query_rope) * factor
    return grad_query, jnp.concatenate([grad_key, grad_value], axis=-1), grad_rope


def reference(query, kv_latent, kv_weight, grad_out, doc_lengths):
    factor = (NOPE + ROPE) ** -0.5
    kv_width = NOPE + VDIM
    columns = LATENT + ROPE
    window_rows = TOK_CTX + DOC_MAX
    query_grads = []
    latent_grads = []
    weight_grad = jnp.zeros((LATENT, HEADS * kv_width), jnp.float32)
    for replica in range(REPLICAS):
        padded = jnp.concatenate([jnp.zeros((DOC_MAX, columns), kv_latent.dtype), kv_latent[replica]], axis=0)
        kv_rows = jnp.dot(padded[:, :LATENT], kv_weight, preferred_element_type=jnp.float32).astype(jnp.bfloat16)
        kv_rows = kv_rows.reshape(TOKENS + DOC_MAX, HEADS, kv_width)
        key_nope = kv_rows[..., :NOPE]
        value_rows = kv_rows[..., NOPE:]
        key_rope = padded[:, LATENT:]
        lengths = doc_lengths[replica]
        starts = jnp.cumsum(lengths) - lengths
        positions = jnp.arange(TOKENS + DOC_MAX, dtype=jnp.int32) - DOC_MAX
        doc_ids = jnp.sum((positions[:, None] >= starts[None, :]).astype(jnp.int32), axis=1) - 1
        queries = query[replica].reshape(TOKENS, HEADS, NOPE + ROPE)
        upstream = grad_out[replica].reshape(TOKENS, HEADS, VDIM)
        latent_grad = jnp.zeros((TOKENS + DOC_MAX, columns), jnp.float32)
        pieces = []
        for group in range(N_CTX):
            group_start = group * TOK_CTX
            accum_kv = jnp.zeros((window_rows, HEADS, kv_width), jnp.float32)
            accum_rope = jnp.zeros((window_rows, ROPE), jnp.float32)
            for block_number in range(TOK_CTX // BLOCK):
                start = group_start + block_number * BLOCK
                key_end = start + DOC_MAX + BLOCK
                grad_query, grad_kv, grad_rope = attend(
                    queries[start:start + BLOCK], upstream[start:start + BLOCK],
                    key_nope[start:key_end], key_rope[start:key_end], value_rows[start:key_end],
                    doc_ids[start + DOC_MAX:key_end], doc_ids[start:key_end],
                    positions[start + DOC_MAX:key_end], positions[start:key_end], factor)
                pieces.append(grad_query)
                offset = block_number * BLOCK
                accum_kv = accum_kv.at[offset:offset + DOC_MAX + BLOCK].add(grad_kv)
                accum_rope = accum_rope.at[offset:offset + DOC_MAX + BLOCK].add(grad_rope)
            key_grads = accum_kv.astype(jnp.bfloat16).reshape(window_rows, HEADS * kv_width)
            latent_rows = padded[group_start:group_start + window_rows, :LATENT]
            weight_grad = weight_grad + jnp.dot(latent_rows.T, key_grads, preferred_element_type=jnp.float32)
            latent_term = jnp.concatenate([jnp.dot(key_grads, kv_weight.T, preferred_element_type=jnp.float32), accum_rope], axis=1)
            latent_grad = latent_grad.at[group_start:group_start + window_rows].add(latent_term)
        query_grads.append(jnp.concatenate(pieces, axis=0).reshape(TOKENS, HEADS * (NOPE + ROPE)))
        latent_grads.append(latent_grad[DOC_MAX:].astype(jnp.bfloat16))
    return jnp.stack(query_grads), jnp.stack(latent_grads), weight_grad
```

```python
import jax
import jax.numpy as jnp
from jax import lax
from jax.sharding import PartitionSpec as P

LATENT = 512
ROPE = 64
NOPE = 128
VDIM = 128
HEADS_DEV = 4
TOK_CTX = 512
DOC_MAX = 512
BLOCK = 512
TILE = 128
N_CTX = 4
HEAD_DEVS = 32


def passed_along(array, axis, by):
    length = lax.axis_size(axis)
    pairs = [(i, i + by) for i in range(length) if 0 <= i + by < length]
    return lax.ppermute(array, axis, pairs)


def shift_pairs(by):
    return [(i, (i + by) % N_CTX) for i in range(N_CTX)]


def gathered_rows(rows):
    copies = jnp.broadcast_to(rows[None], (HEAD_DEVS, *rows.shape))
    return lax.all_to_all(copies, "head", 0, 0).reshape(-1, rows.shape[-1])


def summed_weight(part):
    core = lax.axis_index("dp")
    place = lax.axis_index("ctx")
    half, quarter = LATENT // 2, LATENT // 8
    swap = [(0, 1), (1, 0)]
    low = part.astype(jnp.bfloat16)
    other = lax.ppermute(lax.dynamic_slice_in_dim(low, (1 - core) * half, half), "dp", swap)
    mine = lax.dynamic_slice_in_dim(part, core * half, half) + other.astype(jnp.float32)
    low = mine.astype(jnp.bfloat16)
    total = lax.dynamic_slice_in_dim(mine, place * quarter, quarter)
    for by in range(1, N_CTX):
        chunk = lax.dynamic_slice_in_dim(low, (place + by) % N_CTX * quarter, quarter)
        total = total + lax.ppermute(chunk, "ctx", shift_pairs(by)).astype(jnp.float32)
    low = total.astype(jnp.bfloat16)
    pieces = [low] + [lax.ppermute(low, "ctx", shift_pairs(by)) for by in range(1, N_CTX)]
    line = jnp.concatenate(pieces[::-1] + pieces[:0:-1], axis=0)
    mine = lax.dynamic_slice_in_dim(line, (N_CTX - 1 - place) * quarter, half)
    other = lax.ppermute(mine, "dp", swap)
    line = jnp.concatenate([mine, other, mine], axis=0)
    return lax.dynamic_slice_in_dim(line, core * half, LATENT).astype(jnp.float32)


def attend(
    query_block,
    grad_block,
    key_nope,
    key_rope,
    value_rows,
    query_doc,
    key_doc,
    query_pos,
    key_pos,
    factor,
):
    query_nope = query_block[..., :NOPE]
    query_rope = query_block[..., NOPE:]
    scores = (
        jnp.einsum("qhd,khd->hqk", query_nope, key_nope, preferred_element_type=jnp.float32)
        + jnp.einsum("qhd,kd->hqk", query_rope, key_rope, preferred_element_type=jnp.float32)
    ) * factor
    allowed = (query_doc[:, None] == key_doc[None, :]) & (key_pos[None, :] <= query_pos[:, None])
    scores = jnp.where(allowed[None], scores, -1e30)
    top_score = jnp.max(scores, axis=-1, keepdims=True)
    weights = jnp.where(allowed[None], jnp.exp(scores - top_score), 0.0)
    prob = weights / jnp.sum(weights, axis=-1, keepdims=True)
    prob_low = prob.astype(jnp.bfloat16)
    output = jnp.einsum("hqk,khd->qhd", prob_low, value_rows, preferred_element_type=jnp.float32)
    delta = jnp.sum(grad_block.astype(jnp.float32) * output, axis=-1)
    dots = jnp.einsum("qhd,khd->hqk", grad_block, value_rows, preferred_element_type=jnp.float32)
    slope = (prob * (dots - delta.T[:, :, None])).astype(jnp.bfloat16)
    grad_nope = (
        jnp.einsum("hqk,khd->qhd", slope, key_nope, preferred_element_type=jnp.float32) * factor
    )
    grad_rot = (
        jnp.einsum("hqk,kd->qhd", slope, key_rope, preferred_element_type=jnp.float32) * factor
    )
    grad_query = jnp.concatenate([grad_nope, grad_rot], axis=-1).astype(jnp.bfloat16)
    grad_key = (
        jnp.einsum("hqk,qhd->khd", slope, query_nope, preferred_element_type=jnp.float32) * factor
    )
    grad_value = jnp.einsum(
        "hqk,qhd->khd", prob_low, grad_block, preferred_element_type=jnp.float32
    )
    grad_rope = (
        jnp.einsum("hqk,qhd->kd", slope, query_rope, preferred_element_type=jnp.float32) * factor
    )
    return (grad_query, jnp.concatenate([grad_key, grad_value], axis=-1), grad_rope)


def on_device(query, kv_latent, kv_weight, grad_out, doc_lengths):
    factor = (NOPE + ROPE) ** (-0.5)
    kv_width = NOPE + VDIM
    window_rows = TOK_CTX + DOC_MAX
    back_tiles = DOC_MAX // TILE
    own_all = gathered_rows(kv_latent[0])
    prev_all = passed_along(own_all, "ctx", 1)
    window = jnp.concatenate([prev_all, own_all], axis=0)
    kv_rows = jnp.dot(window[:, :LATENT], kv_weight, preferred_element_type=jnp.float32).astype(
        jnp.bfloat16
    )
    kv_rows = kv_rows.reshape(window_rows, HEADS_DEV, kv_width)
    key_nope = kv_rows[..., :NOPE]
    value_rows = kv_rows[..., NOPE:]
    key_rope = window[:, LATENT:]
    ctx_pos = lax.axis_index("ctx")
    lengths = doc_lengths[0]
    starts = jnp.cumsum(lengths) - lengths
    positions = ctx_pos * TOK_CTX - DOC_MAX + jnp.arange(window_rows, dtype=jnp.int32)
    doc_ids = jnp.sum((positions[:, None] >= starts[None, :]).astype(jnp.int32), axis=1) - 1
    offsets = jnp.arange(window_rows, dtype=jnp.int32)
    queries = query[0].reshape(TOK_CTX, HEADS_DEV, NOPE + ROPE)
    upstream = grad_out[0].reshape(TOK_CTX, HEADS_DEV, VDIM)
    accum_kv = jnp.zeros((window_rows, HEADS_DEV, kv_width), jnp.float32)
    accum_rope = jnp.zeros((window_rows, ROPE), jnp.float32)
    key_lower = DOC_MAX - back_tiles * TILE
    key_upper = DOC_MAX + BLOCK
    grad_query, grad_kv, grad_rope = attend(
        queries,
        upstream,
        key_nope,
        key_rope,
        value_rows,
        doc_ids[DOC_MAX:key_upper],
        doc_ids,
        offsets[DOC_MAX:key_upper],
        offsets,
        factor,
    )
    accum_kv, accum_rope, grad_query = (
        accum_kv.at[key_lower:key_upper].add(grad_kv),
        accum_rope.at[key_lower:key_upper].add(grad_rope),
        grad_query,
    )
    d_query = grad_query.reshape(1, TOK_CTX, HEADS_DEV * (NOPE + ROPE))
    key_grads = accum_kv.astype(jnp.bfloat16).reshape(window_rows, HEADS_DEV * kv_width)
    weight_part = jnp.dot(window[:, :LATENT].T, key_grads, preferred_element_type=jnp.float32)
    d_kv_weight = summed_weight(weight_part)
    latent_term = jnp.concatenate(
        [jnp.dot(key_grads, kv_weight.T, preferred_element_type=jnp.float32), accum_rope], axis=1
    )
    incoming = passed_along(latent_term[:DOC_MAX].astype(jnp.bfloat16), "ctx", -1).astype(
        jnp.float32
    )
    own_term = latent_term[DOC_MAX:].at[TOK_CTX - DOC_MAX :].add(incoming)
    terms = lax.all_to_all(
        own_term.astype(jnp.bfloat16).reshape(HEAD_DEVS, -1, LATENT + ROPE), "head", 0, 0
    )
    summed = jnp.sum(terms.astype(jnp.float32), axis=0)
    d_latent = summed.astype(jnp.bfloat16)[None]
    return (d_query, d_latent, d_kv_weight)


def solution(mesh):
    return jax.shard_map(
        on_device,
        mesh=mesh,
        in_specs=(
            P("dp", "ctx", "head"),
            P("dp", ("ctx", "head"), None),
            P(None, "head"),
            P("dp", "ctx", "head"),
            P("dp", None),
        ),
        out_specs=(P("dp", "ctx", "head"), P("dp", ("ctx", "head"), None), P(None, "head")),
        check_vma=False,
    )
```

```python
import jax
import jax.numpy as jnp
from jax import lax
from jax.experimental import pallas as pl
from jax.experimental.pallas import tpu as pltpu
from jax.sharding import PartitionSpec as P

LATENT = 512
ROPE = 64
NOPE = 128
VDIM = 128
HEADS_DEV = 4
TOK_CTX = 512
DOC_MAX = 512
QUERIES = 256
KEYS = QUERIES + DOC_MAX
WINDOW = TOK_CTX + DOC_MAX
KV_WIDTH = NOPE + VDIM
FACTOR = (NOPE + ROPE) ** -0.5
LOG2E = 1.4426950408889634
N_CTX = 4
HEAD_DEVS = 32


def passed_along(array, axis, by):
    length = lax.axis_size(axis)
    pairs = [(i, i + by) for i in range(length) if 0 <= i + by < length]
    return lax.ppermute(array, axis, pairs)


def shift_pairs(by):
    return [(i, (i + by) % N_CTX) for i in range(N_CTX)]


def gathered_rows(rows):
    copies = jnp.broadcast_to(rows[None], (HEAD_DEVS, *rows.shape))
    return lax.all_to_all(copies, "head", 0, 0).reshape(-1, rows.shape[-1])


def summed_weight(part):
    core = lax.axis_index("dp")
    place = lax.axis_index("ctx")
    half, quarter = LATENT // 2, LATENT // 8
    swap = [(0, 1), (1, 0)]
    low = part
    other = lax.ppermute(lax.dynamic_slice_in_dim(low, (1 - core) * half, half), "dp", swap)
    mine = lax.dynamic_slice_in_dim(low, core * half, half).astype(jnp.float32)
    mine = mine + other.astype(jnp.float32)
    low = mine.astype(jnp.bfloat16)
    total = lax.dynamic_slice_in_dim(mine, place * quarter, quarter)
    for by in range(1, N_CTX):
        chunk = lax.dynamic_slice_in_dim(low, (place + by) % N_CTX * quarter, quarter)
        total = total + lax.ppermute(chunk, "ctx", shift_pairs(by)).astype(jnp.float32)
    low = total.astype(jnp.bfloat16)
    pieces = [low] + [lax.ppermute(low, "ctx", shift_pairs(by)) for by in range(1, N_CTX)]
    line = jnp.concatenate(pieces[::-1] + pieces[:0:-1], axis=0)
    mine = lax.dynamic_slice_in_dim(line, (N_CTX - 1 - place) * quarter, half)
    other = lax.ppermute(mine, "dp", swap)
    line = jnp.concatenate([mine, other, mine], axis=0)
    return lax.dynamic_slice_in_dim(line, core * half, LATENT).astype(jnp.float32)


NT = (((1,), (1,)), ((), ()))
NN = (((1,), (0,)), ((), ()))
TN = (((0,), (0,)), ((), ()))


def mm(left, right, dims):
    return lax.dot_general(left, right, dims, preferred_element_type=jnp.float32)


def attention_kernel(
    low_ref,
    prev_ref,
    own_ref,
    weight_ref,
    query_ref,
    grad_ref,
    d_query_ref,
    d_weight_ref,
    prev_term_ref,
    own_term_ref,
    bias_ref,
    turned_ref,
    term_ref,
    rope_ref,
):
    step = pl.program_id(0)
    low = jnp.bfloat16
    rows = jnp.concatenate([prev_ref[...], own_ref[...]], axis=0)
    latent = rows[:, :LATENT]
    key_rope = rows[:, LATENT:]
    blank = jnp.zeros((WINDOW, ROPE), low)

    @pl.when(step == 0)
    def _():
        turned_ref[...] = latent.T
        term_ref[...] = jnp.zeros_like(term_ref)
        rope_ref[...] = jnp.zeros_like(rope_ref)
        for tile in range(TOK_CTX // QUERIES):
            first = tile * QUERIES
            key = first + lax.broadcasted_iota(jnp.int32, (KEYS, QUERIES), 0)
            query = first + DOC_MAX + lax.broadcasted_iota(jnp.int32, (KEYS, QUERIES), 1)
            start = low_ref[:, first : first + QUERIES]
            allowed = (key >= start) & (key <= query)
            bias_ref[tile] = jnp.where(allowed, 0.0, -1e30)

    middle = []
    for head in range(2):
        head_weight = weight_ref[:, head * KV_WIDTH : (head + 1) * KV_WIDTH]
        kv_rows = mm(latent, head_weight, NN).astype(low)
        key_nope = kv_rows[:, :NOPE]
        value_rows = kv_rows[:, NOPE:]
        parts = [key_nope, key_rope, blank] if head == 0 else [blank, key_nope, key_rope]
        keys = jnp.concatenate(parts, axis=1)
        grads = []
        for tile in range(TOK_CTX // QUERIES):
            first = tile * QUERIES
            queries = query_ref[first : first + QUERIES, head * NOPE : head * NOPE + 2 * NOPE]
            upstream = grad_ref[first : first + QUERIES, head * VDIM : (head + 1) * VDIM]
            tile_keys = keys[first : first + KEYS]
            tile_values = value_rows[first : first + KEYS]
            scores = mm(tile_keys, queries, NT) * (FACTOR * LOG2E) + bias_ref[tile]
            weights = jnp.exp2(scores - jnp.max(scores, axis=0, keepdims=True))
            prob = weights * (1.0 / jnp.sum(weights, axis=0, keepdims=True))
            prob_low = prob.astype(low)
            dots = mm(tile_values, upstream, NT)
            delta = jnp.sum(prob_low.astype(jnp.float32) * dots, axis=0, keepdims=True)
            slope = (prob * (dots - delta)).astype(low)
            grads.append((mm(slope, queries, NN), mm(prob_low, upstream, NN)))
            d_query = mm(slope, tile_keys, TN) * FACTOR
            at = slice(first, first + QUERIES)
            if head == 0:
                d_query_ref[at, :NOPE] = d_query[:, :NOPE].astype(low)
                middle.append(d_query[:, NOPE:])
            else:
                d_query_ref[at, NOPE : 2 * NOPE] = (middle[tile] + d_query[:, :NOPE]).astype(low)
                d_query_ref[at, 2 * NOPE :] = d_query[:, NOPE:].astype(low)
        key_grad, value_grad = (
            jnp.concatenate(
                [one[:QUERIES], one[QUERIES:] + two[:-QUERIES], two[-QUERIES:]], axis=0
            )
            for one, two in zip(*grads)
        )
        key_grad = key_grad * FACTOR
        if head == 0:
            nope_grad, rope_grad = key_grad[:, :NOPE], key_grad[:, NOPE : NOPE + ROPE]
        else:
            nope_grad, rope_grad = key_grad[:, ROPE : ROPE + NOPE], key_grad[:, ROPE + NOPE :]
        rope_ref[...] += rope_grad
        kv_grad = jnp.concatenate([nope_grad.astype(low), value_grad.astype(low)], axis=1)
        d_weight_ref[:, head * KV_WIDTH : (head + 1) * KV_WIDTH] = mm(
            turned_ref[...], kv_grad, NN
        ).astype(low)
        term_ref[...] += mm(kv_grad, head_weight, NT)

    @pl.when(step == pl.num_programs(0) - 1)
    def _():
        prev_term_ref[:, :LATENT] = term_ref[:DOC_MAX].astype(low)
        prev_term_ref[:, LATENT:] = rope_ref[:DOC_MAX].astype(low)
        own_term_ref[:, :LATENT] = term_ref[DOC_MAX:]
        own_term_ref[:, LATENT:] = rope_ref[DOC_MAX:]


def attention(low_keys, prev_rows, own_rows, weight, query, grad_out):
    def whole(shape):
        return pl.BlockSpec(shape, lambda step: (0, 0))

    def columns(count, width):
        return pl.BlockSpec((count, width), lambda step: (0, step))

    columns_latent = LATENT + ROPE
    return pl.pallas_call(
        attention_kernel,
        grid=(HEADS_DEV // 2,),
        in_specs=[
            whole((1, TOK_CTX)),
            whole((DOC_MAX, columns_latent)),
            whole((TOK_CTX, columns_latent)),
            columns(LATENT, 2 * KV_WIDTH),
            columns(TOK_CTX, 2 * (NOPE + ROPE)),
            columns(TOK_CTX, 2 * VDIM),
        ],
        out_specs=[
            columns(TOK_CTX, 2 * (NOPE + ROPE)),
            columns(LATENT, 2 * KV_WIDTH),
            whole((DOC_MAX, columns_latent)),
            whole((TOK_CTX, columns_latent)),
        ],
        out_shape=[
            jax.ShapeDtypeStruct((TOK_CTX, HEADS_DEV * (NOPE + ROPE)), jnp.bfloat16),
            jax.ShapeDtypeStruct((LATENT, HEADS_DEV * KV_WIDTH), jnp.bfloat16),
            jax.ShapeDtypeStruct((DOC_MAX, columns_latent), jnp.bfloat16),
            jax.ShapeDtypeStruct((TOK_CTX, columns_latent), jnp.float32),
        ],
        scratch_shapes=[
            pltpu.VMEM((TOK_CTX // QUERIES, KEYS, QUERIES), jnp.float32),
            pltpu.VMEM((LATENT, WINDOW), jnp.bfloat16),
            pltpu.VMEM((WINDOW, LATENT), jnp.float32),
            pltpu.VMEM((WINDOW, ROPE), jnp.float32),
        ],
        compiler_params=pltpu.CompilerParams(vmem_limit_bytes=48 * 1024 * 1024),
        cost_estimate=pl.CostEstimate(
            flops=8_000_000_000, bytes_accessed=10_000_000, transcendentals=1_600_000
        ),
        name="attention",
    )(low_keys, prev_rows, own_rows, weight, query, grad_out)


def first_keys(lengths):
    starts = jnp.cumsum(lengths) - lengths
    base = lax.axis_index("ctx") * TOK_CTX
    positions = base + jnp.arange(TOK_CTX, dtype=jnp.int32)
    reached = jnp.where(starts[:, None] <= positions[None, :], starts[:, None], 0)
    return jnp.max(reached, axis=0, keepdims=True) - (base - DOC_MAX)


def on_device(query, kv_latent, kv_weight, grad_out, doc_lengths):
    own_rows = gathered_rows(kv_latent[0])
    prev_rows = passed_along(own_rows, "ctx", 1)
    d_query, weight_part, prev_term, own_term = attention(
        first_keys(doc_lengths[0]), prev_rows, own_rows, kv_weight, query[0], grad_out[0]
    )
    incoming = passed_along(prev_term, "ctx", -1)
    own_term = (own_term + incoming.astype(jnp.float32)).astype(jnp.bfloat16)
    terms = lax.all_to_all(own_term.reshape(HEAD_DEVS, -1, LATENT + ROPE), "head", 0, 0)
    d_latent = jnp.sum(terms.astype(jnp.float32), axis=0).astype(jnp.bfloat16)
    d_kv_weight = summed_weight(weight_part)
    return (d_query[None], d_latent[None], d_kv_weight)


def solution(mesh):
    return jax.shard_map(
        on_device,
        mesh=mesh,
        in_specs=(
            P("dp", "ctx", "head"),
            P("dp", ("ctx", "head"), None),
            P(None, "head"),
            P("dp", "ctx", "head"),
            P("dp", None),
        ),
        out_specs=(P("dp", "ctx", "head"), P("dp", ("ctx", "head"), None), P(None, "head")),
        check_vma=False,
    )
```

```python
import jax
import jax.numpy as jnp
from jax import lax
from jax.experimental import pallas as pl
from jax.experimental.pallas import tpu as pltpu
from jax.sharding import PartitionSpec as P

LATENT = 512
ROPE = 64
NOPE = 128
VDIM = 128
HEADS_DEV = 4
TOK_CTX = 512
DOC_MAX = 512
QUERIES = 256
KEYS = QUERIES + DOC_MAX
WINDOW = TOK_CTX + DOC_MAX
KV_WIDTH = NOPE + VDIM
FACTOR = (NOPE + ROPE) ** -0.5
LOG2E = 1.4426950408889634
N_CTX = 4
Y = 4
Z = 8
ROWS = 16
PART = LATENT // 8


def passed_along(array, by):
    pairs = [(i, i + by) for i in range(N_CTX) if 0 <= i + by < N_CTX]
    return lax.ppermute(array, "ctx", pairs)


def turned(array, axis, by):
    if axis == "ctx":
        return lax.ppermute(array, axis, [(i, (i + by) % N_CTX) for i in range(N_CTX)])
    pairs = [(i, i // Y * Y + (i + by) % Y) for i in range(Z * Y)]
    return lax.ppermute(array, axis, pairs)


def summed_weight(kept, given):
    low = jnp.bfloat16
    swap = [(0, 1), (1, 0)]
    other = lax.ppermute(given, "dp", swap)
    mine = [
        kept[by * PART : (by + 1) * PART].astype(jnp.float32)
        + other[by * PART : (by + 1) * PART].astype(jnp.float32)
        for by in range(N_CTX)
    ]
    total = mine[0]
    for by in range(1, N_CTX):
        total = total + turned(mine[by].astype(low), "ctx", by).astype(jnp.float32)
    total = total.astype(low)
    pieces = [total] + [turned(total, "ctx", by) for by in range(1, N_CTX)]
    pieces = jnp.stack(pieces)
    return placed(pieces, lax.ppermute(pieces, "dp", swap))


def place_kernel(core_ref, place_ref, mine_ref, other_ref, out_ref):
    core, place = core_ref[0], place_ref[0]
    for by in range(N_CTX):
        at = lax.rem(place - by + N_CTX, N_CTX)
        out_ref[core * N_CTX + at] = mine_ref[by].astype(jnp.float32)
        out_ref[(1 - core) * N_CTX + at] = other_ref[by].astype(jnp.float32)


def place_of(axis):
    return lax.axis_index(axis).astype(jnp.int32).reshape(1)


def placed(mine, other):
    vmem = pl.BlockSpec(memory_space=pltpu.VMEM)
    smem = pl.BlockSpec(memory_space=pltpu.SMEM)
    whole = pl.pallas_call(
        place_kernel,
        in_specs=[smem, smem, vmem, vmem],
        out_specs=vmem,
        out_shape=jax.ShapeDtypeStruct((2 * N_CTX, *mine.shape[1:]), jnp.float32),
        compiler_params=pltpu.CompilerParams(vmem_limit_bytes=16 * 1024 * 1024),
        name="placed",
    )(place_of("dp"), place_of("ctx"), mine, other)
    return whole.reshape(LATENT, -1)


NT = (((1,), (1,)), ((), ()))
NN = (((1,), (0,)), ((), ()))
TN = (((0,), (0,)), ((), ()))


def mm(left, right, dims):
    return lax.dot_general(left, right, dims, preferred_element_type=jnp.float32)


def attention_kernel(
    spot_ref,
    low_ref,
    piece0_ref,
    piece1_ref,
    piece2_ref,
    piece3_ref,
    weight_ref,
    query_ref,
    grad_ref,
    d_query_ref,
    kept_ref,
    given_ref,
    term0_ref,
    term1_ref,
    term2_ref,
    term3_ref,
    rows_ref,
    bias_ref,
    plain_ref,
    turned_ref,
    term_ref,
    rope_ref,
):
    step = pl.program_id(0)
    low = jnp.bfloat16
    core, place, spot = spot_ref[0], spot_ref[1], spot_ref[2]

    @pl.when(step == 0)
    def _():
        for by, piece in enumerate([piece0_ref, piece1_ref, piece2_ref, piece3_ref]):
            at = lax.rem(spot - by + Y, Y)
            rows_ref[:Z, at] = piece[:, 0]
            rows_ref[Z:, at] = piece[:, 1]

    rows = rows_ref[...].reshape(WINDOW, LATENT + ROPE)
    latent = rows[:, :LATENT]
    key_rope = rows[:, LATENT:]
    blank = jnp.zeros((WINDOW, ROPE), low)

    @pl.when(step == 0)
    def _():
        plain_ref[...] = latent.T.reshape(2 * N_CTX, PART, WINDOW)
        for by in range(N_CTX):
            at = lax.rem(place + by, N_CTX)
            turned_ref[by] = plain_ref[core * N_CTX + at]
            turned_ref[N_CTX + by] = plain_ref[(1 - core) * N_CTX + at]
        term_ref[...] = jnp.zeros_like(term_ref)
        rope_ref[...] = jnp.zeros_like(rope_ref)
        for tile in range(TOK_CTX // QUERIES):
            first = tile * QUERIES
            key = first + lax.broadcasted_iota(jnp.int32, (KEYS, QUERIES), 0)
            query = first + DOC_MAX + lax.broadcasted_iota(jnp.int32, (KEYS, QUERIES), 1)
            start = low_ref[:, first : first + QUERIES]
            allowed = (key >= start) & (key <= query)
            bias_ref[tile] = jnp.where(allowed, 0.0, -1e30)

    middle = []
    for head in range(2):
        head_weight = weight_ref[:, head * KV_WIDTH : (head + 1) * KV_WIDTH]
        kv_rows = mm(latent, head_weight, NN).astype(low)
        key_nope = kv_rows[:, :NOPE]
        value_rows = kv_rows[:, NOPE:]
        parts = [key_nope, key_rope, blank] if head == 0 else [blank, key_nope, key_rope]
        keys = jnp.concatenate(parts, axis=1)
        grads = []
        for tile in range(TOK_CTX // QUERIES):
            first = tile * QUERIES
            queries = query_ref[first : first + QUERIES, head * NOPE : head * NOPE + 2 * NOPE]
            upstream = grad_ref[first : first + QUERIES, head * VDIM : (head + 1) * VDIM]
            tile_keys = keys[first : first + KEYS]
            tile_values = value_rows[first : first + KEYS]
            scores = mm(tile_keys, queries, NT) * (FACTOR * LOG2E) + bias_ref[tile]
            weights = jnp.exp2(scores - jnp.max(scores, axis=0, keepdims=True))
            prob = weights * (1.0 / jnp.sum(weights, axis=0, keepdims=True))
            prob_low = prob.astype(low)
            dots = mm(tile_values, upstream, NT)
            delta = jnp.sum(prob_low.astype(jnp.float32) * dots, axis=0, keepdims=True)
            slope = (prob * (dots - delta)).astype(low)
            grads.append((mm(slope, queries, NN), mm(prob_low, upstream, NN)))
            d_query = mm(slope, tile_keys, TN) * FACTOR
            at = slice(first, first + QUERIES)
            if head == 0:
                d_query_ref[at, :NOPE] = d_query[:, :NOPE].astype(low)
                middle.append(d_query[:, NOPE:])
            else:
                d_query_ref[at, NOPE : 2 * NOPE] = (middle[tile] + d_query[:, :NOPE]).astype(low)
                d_query_ref[at, 2 * NOPE :] = d_query[:, NOPE:].astype(low)
        key_grad, value_grad = (
            jnp.concatenate(
                [one[:QUERIES], one[QUERIES:] + two[:-QUERIES], two[-QUERIES:]], axis=0
            )
            for one, two in zip(*grads)
        )
        key_grad = key_grad * FACTOR
        if head == 0:
            nope_grad, rope_grad = key_grad[:, :NOPE], key_grad[:, NOPE : NOPE + ROPE]
        else:
            nope_grad, rope_grad = key_grad[:, ROPE : ROPE + NOPE], key_grad[:, ROPE + NOPE :]
        rope_ref[...] += rope_grad.reshape(rope_ref.shape)
        kv_grad = jnp.concatenate([nope_grad.astype(low), value_grad.astype(low)], axis=1)
        part = mm(turned_ref[...].reshape(LATENT, WINDOW), kv_grad, NN).astype(low)
        kept_ref[:, head * KV_WIDTH : (head + 1) * KV_WIDTH] = part[: LATENT // 2]
        given_ref[:, head * KV_WIDTH : (head + 1) * KV_WIDTH] = part[LATENT // 2 :]
        term_ref[...] += mm(kv_grad, head_weight, NT).reshape(term_ref.shape)

    @pl.when(step == pl.num_programs(0) - 1)
    def _():
        for by, out in enumerate([term0_ref, term1_ref, term2_ref, term3_ref]):
            at = lax.rem(spot + by, Y)
            term, rope = term_ref[:, at].astype(out.dtype), rope_ref[:, at].astype(out.dtype)
            for half in range(2):
                out[:, half, :, :LATENT] = term[half * Z : (half + 1) * Z]
                out[:, half, :, LATENT:] = rope[half * Z : (half + 1) * Z]


def attention(spot, low_keys, pieces, weight, query, grad_out):
    def whole(shape):
        return pl.BlockSpec(shape, lambda step: (0,) * len(shape))

    def columns(count, width):
        return pl.BlockSpec((count, width), lambda step: (0, step))

    piece = (Z, 2, ROWS, LATENT + ROPE)
    return pl.pallas_call(
        attention_kernel,
        grid=(HEADS_DEV // 2,),
        in_specs=[
            pl.BlockSpec(memory_space=pltpu.SMEM),
            whole((1, TOK_CTX)),
            *[whole(piece)] * Y,
            columns(LATENT, 2 * KV_WIDTH),
            columns(TOK_CTX, 2 * (NOPE + ROPE)),
            columns(TOK_CTX, 2 * VDIM),
        ],
        out_specs=[
            columns(TOK_CTX, 2 * (NOPE + ROPE)),
            columns(LATENT // 2, 2 * KV_WIDTH),
            columns(LATENT // 2, 2 * KV_WIDTH),
            *[whole(piece)] * Y,
        ],
        out_shape=[
            jax.ShapeDtypeStruct((TOK_CTX, HEADS_DEV * (NOPE + ROPE)), jnp.bfloat16),
            jax.ShapeDtypeStruct((LATENT // 2, HEADS_DEV * KV_WIDTH), jnp.bfloat16),
            jax.ShapeDtypeStruct((LATENT // 2, HEADS_DEV * KV_WIDTH), jnp.bfloat16),
            jax.ShapeDtypeStruct(piece, jnp.float32),
            *[jax.ShapeDtypeStruct(piece, jnp.bfloat16)] * (Y - 1),
        ],
        scratch_shapes=[
            pltpu.VMEM((2 * Z, Y, ROWS, LATENT + ROPE), jnp.bfloat16),
            pltpu.VMEM((TOK_CTX // QUERIES, KEYS, QUERIES), jnp.float32),
            pltpu.VMEM((2 * N_CTX, PART, WINDOW), jnp.bfloat16),
            pltpu.VMEM((2 * N_CTX, PART, WINDOW), jnp.bfloat16),
            pltpu.VMEM((2 * Z, Y, ROWS, LATENT), jnp.float32),
            pltpu.VMEM((2 * Z, Y, ROWS, ROPE), jnp.float32),
        ],
        compiler_params=pltpu.CompilerParams(vmem_limit_bytes=48 * 1024 * 1024),
        cost_estimate=pl.CostEstimate(
            flops=8_000_000_000, bytes_accessed=10_000_000, transcendentals=1_600_000
        ),
        name="attention",
    )(spot, low_keys, *pieces, weight, query, grad_out)


def first_keys(lengths):
    starts = jnp.cumsum(lengths) - lengths
    base = lax.axis_index("ctx") * TOK_CTX
    positions = base + jnp.arange(TOK_CTX, dtype=jnp.int32)
    reached = jnp.where(starts[:, None] <= positions[None, :], starts[:, None], 0)
    return jnp.max(reached, axis=0, keepdims=True) - (base - DOC_MAX)


def on_device(query, kv_latent, kv_weight, grad_out, doc_lengths):
    along_z = [[z * Y + y for z in range(Z)] for y in range(Y)]
    rows = jnp.stack([passed_along(kv_latent[0], 1), kv_latent[0]])
    rows = lax.all_gather(rows, "head", axis_index_groups=along_z)
    pieces = [rows] + [turned(rows, "head", by) for by in range(1, Y)]
    spot = jnp.stack(
        [lax.axis_index("dp"), lax.axis_index("ctx"), lax.axis_index("head") % Y]
    ).astype(jnp.int32)
    d_query, kept, given, *terms = attention(
        spot, first_keys(doc_lengths[0]), pieces, kv_weight, query[0], grad_out[0]
    )
    term = terms[0]
    for by in range(1, Y):
        term = term + turned(terms[by], "head", by).astype(jnp.float32)
    shares = lax.all_to_all(
        term.astype(jnp.bfloat16), "head", 0, 0, axis_index_groups=along_z
    )
    share = jnp.sum(shares.astype(jnp.float32), axis=0)
    d_latent = share[1] + passed_along(share[0].astype(jnp.bfloat16), -1).astype(jnp.float32)
    d_kv_weight = summed_weight(kept, given)
    return (d_query[None], d_latent.astype(jnp.bfloat16)[None], d_kv_weight)


def solution(mesh):
    return jax.shard_map(
        on_device,
        mesh=mesh,
        in_specs=(
            P("dp", "ctx", "head"),
            P("dp", ("ctx", "head"), None),
            P(None, "head"),
            P("dp", "ctx", "head"),
            P("dp", None),
        ),
        out_specs=(P("dp", "ctx", "head"), P("dp", ("ctx", "head"), None), P(None, "head")),
        check_vma=False,
    )
```

```python
import jax
import jax.numpy as jnp
from jax import lax
from jax.experimental import pallas as pl
from jax.experimental.pallas import tpu as pltpu
from jax.sharding import PartitionSpec as P

LATENT = 512
ROPE = 64
NOPE = 128
VDIM = 128
HEADS_DEV = 4
TOK_CTX = 512
DOC_MAX = 512
QUERIES = 256
KEYS = QUERIES + DOC_MAX
WINDOW = TOK_CTX + DOC_MAX
KV_WIDTH = NOPE + VDIM
FACTOR = (NOPE + ROPE) ** -0.5
LOG2E = 1.4426950408889634
N_CTX = 4
Y = 4
Z = 8
ROWS = 16
PART = LATENT // 8


def passed_along(array, by):
    pairs = [(i, i + by) for i in range(N_CTX) if 0 <= i + by < N_CTX]
    return lax.ppermute(array, "ctx", pairs)


def turned(array, axis, by):
    if axis == "ctx":
        return lax.ppermute(array, axis, [(i, (i + by) % N_CTX) for i in range(N_CTX)])
    pairs = [(i, i // Y * Y + (i + by) % Y) for i in range(Z * Y)]
    return lax.ppermute(array, axis, pairs)


def first_sum_kernel(kept_ref, other_ref, after_ref, mine_ref, *out_refs):
    for by, out in enumerate([mine_ref, *out_refs]):
        at = slice(by * PART, (by + 1) * PART)
        total = kept_ref[at].astype(jnp.float32) + other_ref[at].astype(jnp.float32)
        out[...] = total.astype(out.dtype)


def second_sum_kernel(mine_ref, one_ref, two_ref, three_ref, after_ref, out_ref):
    total = mine_ref[...]
    for ref in (one_ref, two_ref, three_ref):
        total = total + ref[...].astype(jnp.float32)
    out_ref[...] = total.astype(out_ref.dtype)


def stack_kernel(one_ref, two_ref, three_ref, four_ref, after_ref, out_ref):
    for by, ref in enumerate((one_ref, two_ref, three_ref, four_ref)):
        out_ref[by] = ref[...]


def small_call(kernel, out_shape, name, *operands, after):
    vmem = pl.BlockSpec(memory_space=pltpu.VMEM)
    return pl.pallas_call(
        kernel,
        in_specs=[vmem] * len(operands) + [pl.BlockSpec(memory_space=pl.ANY)],
        out_specs=jax.tree.map(lambda _: vmem, out_shape),
        out_shape=out_shape,
        compiler_params=pltpu.CompilerParams(vmem_limit_bytes=16 * 1024 * 1024),
        name=name,
    )(*operands, after)


def summed_weight(kept, given, first_after, second_after):
    swap = [(0, 1), (1, 0)]
    other = lax.ppermute(given, "dp", swap)
    shape = (PART, given.shape[1])
    full = jax.ShapeDtypeStruct(shape, jnp.float32)
    low = jax.ShapeDtypeStruct(shape, jnp.bfloat16)
    mine, *rest = small_call(
        first_sum_kernel, [full, low, low, low], "first_sum", kept, other, after=first_after
    )
    rest = [turned(part, "ctx", by + 1) for by, part in enumerate(rest)]
    total = small_call(second_sum_kernel, low, "second_sum", mine, *rest, after=second_after)
    pieces = [total] + [turned(total, "ctx", by) for by in range(1, N_CTX)]
    return pieces


def place_kernel(core_ref, place_ref, mine_ref, other_ref, out_ref):
    core, place = core_ref[0], place_ref[0]
    for by in range(N_CTX):
        at = lax.rem(place - by + N_CTX, N_CTX)
        out_ref[core * N_CTX + at] = mine_ref[by].astype(jnp.float32)
        out_ref[(1 - core) * N_CTX + at] = other_ref[by].astype(jnp.float32)


def place_of(axis):
    return lax.axis_index(axis).astype(jnp.int32).reshape(1)


def placed(mine, other):
    vmem = pl.BlockSpec(memory_space=pltpu.VMEM)
    smem = pl.BlockSpec(memory_space=pltpu.SMEM)
    whole = pl.pallas_call(
        place_kernel,
        in_specs=[smem, smem, vmem, vmem],
        out_specs=vmem,
        out_shape=jax.ShapeDtypeStruct((2 * N_CTX, *mine.shape[1:]), jnp.float32),
        compiler_params=pltpu.CompilerParams(vmem_limit_bytes=16 * 1024 * 1024),
        name="placed",
    )(place_of("dp"), place_of("ctx"), mine, other)
    return whole.reshape(LATENT, -1)


NT = (((1,), (1,)), ((), ()))
NN = (((1,), (0,)), ((), ()))
TN = (((0,), (0,)), ((), ()))


def mm(left, right, dims):
    return lax.dot_general(left, right, dims, preferred_element_type=jnp.float32)


def attention_kernel(spot_ref, low_ref, *refs):
    own_pieces, prev_pieces, refs = refs[:Y], refs[Y : 2 * Y], refs[2 * Y :]
    weight_ref, query_ref, grad_ref, d_query_ref, kept_ref, given_ref, *refs = refs
    own_terms, prev_terms, refs = refs[:Y], refs[Y : 2 * Y], refs[2 * Y :]
    rows_ref, bias_ref, plain_ref, turned_ref, term_ref, rope_ref = refs
    step = pl.program_id(0)
    low = jnp.bfloat16
    core, place, spot = spot_ref[0], spot_ref[1], spot_ref[2]

    @pl.when(step == 0)
    def _():
        for by in range(Y):
            at = lax.rem(spot - by + Y, Y)
            rows_ref[:Z, at] = prev_pieces[by][...]
            rows_ref[Z:, at] = own_pieces[by][...]

    rows = rows_ref[...].reshape(WINDOW, LATENT + ROPE)
    latent = rows[:, :LATENT]
    key_rope = rows[:, LATENT:]
    blank = jnp.zeros((WINDOW, ROPE), low)

    @pl.when(step == 0)
    def _():
        plain_ref[...] = latent.T.reshape(2 * N_CTX, PART, WINDOW)
        for by in range(N_CTX):
            at = lax.rem(place + by, N_CTX)
            turned_ref[by] = plain_ref[core * N_CTX + at]
            turned_ref[N_CTX + by] = plain_ref[(1 - core) * N_CTX + at]
        term_ref[...] = jnp.zeros_like(term_ref)
        rope_ref[...] = jnp.zeros_like(rope_ref)
        for tile in range(TOK_CTX // QUERIES):
            first = tile * QUERIES
            key = first + lax.broadcasted_iota(jnp.int32, (KEYS, QUERIES), 0)
            query = first + DOC_MAX + lax.broadcasted_iota(jnp.int32, (KEYS, QUERIES), 1)
            start = low_ref[:, first : first + QUERIES]
            allowed = (key >= start) & (key <= query)
            bias_ref[tile] = jnp.where(allowed, 0.0, -1e30)

    middle = []
    for head in range(2):
        head_weight = weight_ref[:, head * KV_WIDTH : (head + 1) * KV_WIDTH]
        kv_rows = mm(latent, head_weight, NN).astype(low)
        key_nope = kv_rows[:, :NOPE]
        value_rows = kv_rows[:, NOPE:]
        parts = [key_nope, key_rope, blank] if head == 0 else [blank, key_nope, key_rope]
        keys = jnp.concatenate(parts, axis=1)
        grads = []
        for tile in range(TOK_CTX // QUERIES):
            first = tile * QUERIES
            queries = query_ref[first : first + QUERIES, head * NOPE : head * NOPE + 2 * NOPE]
            upstream = grad_ref[first : first + QUERIES, head * VDIM : (head + 1) * VDIM]
            tile_keys = keys[first : first + KEYS]
            tile_values = value_rows[first : first + KEYS]
            scores = mm(tile_keys, queries, NT) * (FACTOR * LOG2E) + bias_ref[tile]
            weights = jnp.exp2(scores - jnp.max(scores, axis=0, keepdims=True))
            prob = weights * (1.0 / jnp.sum(weights, axis=0, keepdims=True))
            prob_low = prob.astype(low)
            dots = mm(tile_values, upstream, NT)
            delta = jnp.sum(prob_low.astype(jnp.float32) * dots, axis=0, keepdims=True)
            slope = (prob * (dots - delta)).astype(low)
            grads.append((mm(slope, queries, NN), mm(prob_low, upstream, NN)))
            d_query = mm(slope, tile_keys, TN) * FACTOR
            at = slice(first, first + QUERIES)
            if head == 0:
                d_query_ref[at, :NOPE] = d_query[:, :NOPE].astype(low)
                middle.append(d_query[:, NOPE:])
            else:
                d_query_ref[at, NOPE : 2 * NOPE] = (middle[tile] + d_query[:, :NOPE]).astype(low)
                d_query_ref[at, 2 * NOPE :] = d_query[:, NOPE:].astype(low)
        key_grad, value_grad = (
            jnp.concatenate(
                [one[:QUERIES], one[QUERIES:] + two[:-QUERIES], two[-QUERIES:]], axis=0
            )
            for one, two in zip(*grads)
        )
        key_grad = key_grad * FACTOR
        if head == 0:
            nope_grad, rope_grad = key_grad[:, :NOPE], key_grad[:, NOPE : NOPE + ROPE]
        else:
            nope_grad, rope_grad = key_grad[:, ROPE : ROPE + NOPE], key_grad[:, ROPE + NOPE :]
        rope_ref[...] += rope_grad.reshape(rope_ref.shape)
        kv_grad = jnp.concatenate([nope_grad.astype(low), value_grad.astype(low)], axis=1)
        part = mm(turned_ref[...].reshape(LATENT, WINDOW), kv_grad, NN).astype(low)
        kept_ref[:, head * KV_WIDTH : (head + 1) * KV_WIDTH] = part[: LATENT // 2]
        given_ref[:, head * KV_WIDTH : (head + 1) * KV_WIDTH] = part[LATENT // 2 :]
        term_ref[...] += mm(kv_grad, head_weight, NT).reshape(term_ref.shape)

    @pl.when(step == pl.num_programs(0) - 1)
    def _():
        for by in range(Y):
            at = lax.rem(spot + by, Y)
            for outs, first in ((prev_terms, 0), (own_terms, Z)):
                out = outs[by]
                out[:, :, :LATENT] = term_ref[first : first + Z, at].astype(out.dtype)
                out[:, :, LATENT:] = rope_ref[first : first + Z, at].astype(out.dtype)


def attention(spot, low_keys, own_pieces, prev_pieces, weight, query, grad_out):
    def whole(shape):
        return pl.BlockSpec(shape, lambda step: (0,) * len(shape))

    def columns(count, width):
        return pl.BlockSpec((count, width), lambda step: (0, step))

    piece = (Z, ROWS, LATENT + ROPE)
    return pl.pallas_call(
        attention_kernel,
        grid=(HEADS_DEV // 2,),
        in_specs=[
            pl.BlockSpec(memory_space=pltpu.SMEM),
            whole((1, TOK_CTX)),
            *[whole(piece)] * (2 * Y),
            columns(LATENT, 2 * KV_WIDTH),
            columns(TOK_CTX, 2 * (NOPE + ROPE)),
            columns(TOK_CTX, 2 * VDIM),
        ],
        out_specs=[
            columns(TOK_CTX, 2 * (NOPE + ROPE)),
            columns(LATENT // 2, 2 * KV_WIDTH),
            columns(LATENT // 2, 2 * KV_WIDTH),
            *[whole(piece)] * (2 * Y),
        ],
        out_shape=[
            jax.ShapeDtypeStruct((TOK_CTX, HEADS_DEV * (NOPE + ROPE)), jnp.bfloat16),
            jax.ShapeDtypeStruct((LATENT // 2, HEADS_DEV * KV_WIDTH), jnp.bfloat16),
            jax.ShapeDtypeStruct((LATENT // 2, HEADS_DEV * KV_WIDTH), jnp.bfloat16),
            *[jax.ShapeDtypeStruct(piece, jnp.float32 if by == 0 else jnp.bfloat16) for by in range(Y)] * 2,
        ],
        scratch_shapes=[
            pltpu.VMEM((2 * Z, Y, ROWS, LATENT + ROPE), jnp.bfloat16),
            pltpu.VMEM((TOK_CTX // QUERIES, KEYS, QUERIES), jnp.float32),
            pltpu.VMEM((2 * N_CTX, PART, WINDOW), jnp.bfloat16),
            pltpu.VMEM((2 * N_CTX, PART, WINDOW), jnp.bfloat16),
            pltpu.VMEM((2 * Z, Y, ROWS, LATENT), jnp.float32),
            pltpu.VMEM((2 * Z, Y, ROWS, ROPE), jnp.float32),
        ],
        compiler_params=pltpu.CompilerParams(vmem_limit_bytes=48 * 1024 * 1024),
        cost_estimate=pl.CostEstimate(
            flops=8_000_000_000, bytes_accessed=10_000_000, transcendentals=1_600_000
        ),
        name="attention",
    )(spot, low_keys, *own_pieces, *prev_pieces, weight, query, grad_out)


def first_keys(lengths):
    starts = jnp.cumsum(lengths) - lengths
    base = lax.axis_index("ctx") * TOK_CTX
    positions = base + jnp.arange(TOK_CTX, dtype=jnp.int32)
    reached = jnp.where(starts[:, None] <= positions[None, :], starts[:, None], 0)
    return jnp.max(reached, axis=0, keepdims=True) - (base - DOC_MAX)


def summed_over_y(terms):
    total = terms[0]
    for by in range(1, Y):
        total = total + turned(terms[by], "head", by).astype(jnp.float32)
    return total


def on_device(query, kv_latent, kv_weight, grad_out, doc_lengths):
    along_z = [[z * Y + y for z in range(Z)] for y in range(Y)]
    block = jnp.broadcast_to(kv_latent, (Z, ROWS, LATENT + ROPE))
    block = lax.all_to_all(block, "head", 0, 0, axis_index_groups=along_z)
    prev_block = passed_along(block, 1)
    own_pieces = [block] + [turned(block, "head", by) for by in range(1, Y)]
    prev_pieces = [prev_block] + [turned(prev_block, "head", by) for by in range(1, Y)]
    spot = jnp.stack(
        [lax.axis_index("dp"), lax.axis_index("ctx"), lax.axis_index("head") % Y]
    ).astype(jnp.int32)
    d_query, kept, given, *terms = attention(
        spot,
        first_keys(doc_lengths[0]),
        own_pieces,
        prev_pieces,
        kv_weight,
        query[0],
        grad_out[0],
    )
    prev_term = summed_over_y(terms[Y:]).astype(jnp.bfloat16)
    term = summed_over_y(terms[:Y]) + passed_along(prev_term, -1).astype(jnp.float32)
    term = term.astype(jnp.bfloat16)
    parts = summed_weight(kept, given, prev_term, term)
    shares = lax.all_to_all(term, "head", 0, 0, axis_index_groups=along_z)
    d_latent = jnp.sum(shares.astype(jnp.float32), axis=0).astype(jnp.bfloat16)
    stacked = jax.ShapeDtypeStruct((N_CTX, *parts[0].shape), jnp.bfloat16)
    parts = small_call(stack_kernel, stacked, "stacked", *parts, after=d_latent)
    d_kv_weight = placed(parts, lax.ppermute(parts, "dp", [(0, 1), (1, 0)]))
    return (d_query[None], d_latent[None], d_kv_weight)


def solution(mesh):
    return jax.shard_map(
        on_device,
        mesh=mesh,
        in_specs=(
            P("dp", "ctx", "head"),
            P("dp", ("ctx", "head"), None),
            P(None, "head"),
            P("dp", "ctx", "head"),
            P("dp", None),
        ),
        out_specs=(P("dp", "ctx", "head"), P("dp", ("ctx", "head"), None), P(None, "head")),
        check_vma=False,
    )
```

```python
import jax
import jax.numpy as jnp
from jax import lax
from jax.experimental import pallas as pl
from jax.experimental.pallas import tpu as pltpu
from jax.sharding import PartitionSpec as P

LATENT = 512
ROPE = 64
NOPE = 128
VDIM = 128
HEADS_DEV = 4
TOK_CTX = 512
DOC_MAX = 512
QUERIES = 256
AHEAD = 1
BEHIND = 1
KEYS = QUERIES + DOC_MAX
WINDOW = TOK_CTX + DOC_MAX
KV_WIDTH = NOPE + VDIM
FACTOR = (NOPE + ROPE) ** -0.5
LOG2E = 1.4426950408889634
N_CTX = 4
Y = 4
Z = 8
ROWS = 16
PART = LATENT // 8


def passed_along(array, by):
    pairs = [(i, i + by) for i in range(N_CTX) if 0 <= i + by < N_CTX]
    return lax.ppermute(array, "ctx", pairs)


def turned(array, axis, by):
    if axis == "ctx":
        return lax.ppermute(array, axis, [(i, (i + by) % N_CTX) for i in range(N_CTX)])
    pairs = [(i, i // Y * Y + (i + by) % Y) for i in range(Z * Y)]
    return lax.ppermute(array, axis, pairs)


def first_sum_kernel(kept_ref, other_ref, after_ref, mine_ref, *out_refs):
    for by, out in enumerate([mine_ref, *out_refs]):
        at = slice(by * PART, (by + 1) * PART)
        total = kept_ref[at].astype(jnp.float32) + other_ref[at].astype(jnp.float32)
        out[...] = total.astype(out.dtype)


def second_sum_kernel(mine_ref, one_ref, two_ref, three_ref, after_ref, out_ref):
    total = mine_ref[...]
    for ref in (one_ref, two_ref, three_ref):
        total = total + ref[...].astype(jnp.float32)
    out_ref[...] = total.astype(out_ref.dtype)


def stack_kernel(one_ref, two_ref, three_ref, four_ref, after_ref, out_ref):
    for by, ref in enumerate((one_ref, two_ref, three_ref, four_ref)):
        out_ref[by] = ref[...]


def small_call(kernel, out_shape, name, *operands, after):
    vmem = pl.BlockSpec(memory_space=pltpu.VMEM)
    return pl.pallas_call(
        kernel,
        in_specs=[vmem] * len(operands) + [pl.BlockSpec(memory_space=pl.ANY)],
        out_specs=jax.tree.map(lambda _: vmem, out_shape),
        out_shape=out_shape,
        compiler_params=pltpu.CompilerParams(vmem_limit_bytes=16 * 1024 * 1024),
        name=name,
    )(*operands, after)


def summed_weight(kept, given, first_after, second_after):
    swap = [(0, 1), (1, 0)]
    other = lax.ppermute(given, "dp", swap)
    shape = (PART, given.shape[1])
    full = jax.ShapeDtypeStruct(shape, jnp.float32)
    low = jax.ShapeDtypeStruct(shape, jnp.bfloat16)
    mine, *rest = small_call(
        first_sum_kernel, [full, low, low, low], "first_sum", kept, other, after=first_after
    )
    rest = [turned(part, "ctx", by + 1) for by, part in enumerate(rest)]
    total = small_call(second_sum_kernel, low, "second_sum", mine, *rest, after=second_after)
    pieces = [total] + [turned(total, "ctx", by) for by in range(1, N_CTX)]
    return pieces


def place_kernel(core_ref, place_ref, mine_ref, other_ref, out_ref):
    core, place = core_ref[0], place_ref[0]
    for by in range(N_CTX):
        at = lax.rem(place - by + N_CTX, N_CTX)
        out_ref[core * N_CTX + at] = mine_ref[by].astype(jnp.float32)
        out_ref[(1 - core) * N_CTX + at] = other_ref[by].astype(jnp.float32)


def place_of(axis):
    return lax.axis_index(axis).astype(jnp.int32).reshape(1)


def placed(mine, other):
    vmem = pl.BlockSpec(memory_space=pltpu.VMEM)
    smem = pl.BlockSpec(memory_space=pltpu.SMEM)
    whole = pl.pallas_call(
        place_kernel,
        in_specs=[smem, smem, vmem, vmem],
        out_specs=vmem,
        out_shape=jax.ShapeDtypeStruct((2 * N_CTX, *mine.shape[1:]), jnp.float32),
        compiler_params=pltpu.CompilerParams(vmem_limit_bytes=16 * 1024 * 1024),
        name="placed",
    )(place_of("dp"), place_of("ctx"), mine, other)
    return whole.reshape(LATENT, -1)


NT = (((1,), (1,)), ((), ()))
NN = (((1,), (0,)), ((), ()))
TN = (((0,), (0,)), ((), ()))


def mm(left, right, dims):
    return lax.dot_general(left, right, dims, preferred_element_type=jnp.float32)


def attention_kernel(spot_ref, low_ref, *refs):
    own_pieces, prev_pieces, refs = refs[:Y], refs[Y : 2 * Y], refs[2 * Y :]
    weight_ref, query_in, grad_in, d_query_ref, kept_ref, given_ref, *refs = refs
    own_terms, prev_terms, refs = refs[:Y], refs[Y : 2 * Y], refs[2 * Y :]
    rows_ref, bias_ref, plain_ref, turned_ref, term_ref, rope_ref, *refs = refs
    query_all, grad_all, copied = refs
    step = pl.program_id(0)
    low = jnp.bfloat16
    core, place, spot = spot_ref[0], spot_ref[1], spot_ref[2]

    def copies(pair):
        wide, narrow = 2 * (NOPE + ROPE), 2 * VDIM
        return (
            pltpu.make_async_copy(
                query_in.at[:, pair * wide : (pair + 1) * wide], query_all.at[pair], copied.at[pair]
            ),
            pltpu.make_async_copy(
                grad_in.at[:, pair * narrow : (pair + 1) * narrow],
                grad_all.at[pair],
                copied.at[2 + pair],
            ),
        )

    @pl.when(step == 0)
    def _():
        for pair in range(2):
            for copy in copies(pair):
                copy.start()
        for by in range(Y):
            at = lax.rem(spot - by + Y, Y)
            rows_ref[:Z, at] = prev_pieces[by][...]
            rows_ref[Z:, at] = own_pieces[by][...]

    for pair in range(2):

        @pl.when(step == pair)
        def _():
            for copy in copies(pair):
                copy.wait()

    rows = rows_ref[...].reshape(WINDOW, LATENT + ROPE)
    latent = rows[:, :LATENT]
    key_rope = rows[:, LATENT:]
    blank = jnp.zeros((WINDOW, ROPE), low)

    @pl.when(step == 0)
    def _():
        plain_ref[...] = latent.T.reshape(2 * N_CTX, PART, WINDOW)
        for by in range(N_CTX):
            at = lax.rem(place + by, N_CTX)
            turned_ref[by] = plain_ref[core * N_CTX + at]
            turned_ref[N_CTX + by] = plain_ref[(1 - core) * N_CTX + at]
        term_ref[...] = jnp.zeros_like(term_ref)
        rope_ref[...] = jnp.zeros_like(rope_ref)
        for tile in range(TOK_CTX // QUERIES):
            first = tile * QUERIES
            key = first + lax.broadcasted_iota(jnp.int32, (KEYS, QUERIES), 0)
            query = first + DOC_MAX + lax.broadcasted_iota(jnp.int32, (KEYS, QUERIES), 1)
            start = low_ref[:, first : first + QUERIES]
            allowed = (key >= start) & (key <= query)
            bias_ref[tile] = jnp.where(allowed, 0.0, -1e30)

    kv_rows = mm(latent, weight_ref[...], NN).astype(low)
    keys, values = [], []
    for head in range(2):
        key_nope = kv_rows[:, head * KV_WIDTH : head * KV_WIDTH + NOPE]
        parts = [key_nope, key_rope, blank] if head == 0 else [blank, key_nope, key_rope]
        keys.append(jnp.concatenate(parts, axis=1))
        values.append(kv_rows[:, head * KV_WIDTH + NOPE : (head + 1) * KV_WIDTH])
    spans = [(head, tile * QUERIES) for head in range(2) for tile in range(TOK_CTX // QUERIES)]

    def operands(head, first):
        rows_at = slice(first, first + QUERIES)
        queries = query_all[step, rows_at, head * NOPE : head * NOPE + 2 * NOPE]
        return queries, grad_all[step, rows_at, head * VDIM : (head + 1) * VDIM]

    def products(head, first):
        queries, upstream = operands(head, first)
        scores = mm(keys[head][first : first + KEYS], queries, NT)
        return scores, mm(values[head][first : first + KEYS], upstream, NT)

    def slopes(first, scores, dots):
        scores = scores * (FACTOR * LOG2E) + bias_ref[first // QUERIES]
        weights = jnp.exp2(scores - jnp.max(scores, axis=0, keepdims=True))
        prob = weights * (1.0 / jnp.sum(weights, axis=0, keepdims=True))
        prob_low = prob.astype(low)
        delta = jnp.sum(prob_low.astype(jnp.float32) * dots, axis=0, keepdims=True)
        return prob_low, (prob * (dots - delta)).astype(low)

    def gradients(head, first, prob_low, slope):
        queries, upstream = operands(head, first)
        d_query = mm(slope, keys[head][first : first + KEYS], TN) * FACTOR
        at = slice(first, first + QUERIES)
        if head == 0:
            d_query_ref[at, :NOPE] = d_query[:, :NOPE].astype(low)
            middle.append(d_query[:, NOPE:])
        else:
            whole = middle[first // QUERIES] + d_query[:, :NOPE]
            d_query_ref[at, NOPE : 2 * NOPE] = whole.astype(low)
            d_query_ref[at, 2 * NOPE :] = d_query[:, NOPE:].astype(low)
        return mm(slope, queries, NN), mm(prob_low, upstream, NN)

    middle, grads = [], []
    made, held = {}, {}
    count = len(spans)
    for turn in range(-AHEAD, count + BEHIND):
        if turn + AHEAD < count:
            made[turn + AHEAD] = products(*spans[turn + AHEAD])
        if 0 <= turn < count:
            held[turn] = slopes(spans[turn][1], *made.pop(turn))
        if 0 <= turn - BEHIND:
            grads.append(gradients(*spans[turn - BEHIND], *held.pop(turn - BEHIND)))

    kv_grads, rope_grads = [], []
    for head in range(2):
        key_grad, value_grad = (
            jnp.concatenate(
                [one[:QUERIES], one[QUERIES:] + two[:-QUERIES], two[-QUERIES:]], axis=0
            )
            for one, two in zip(*grads[2 * head : 2 * head + 2])
        )
        key_grad = key_grad * FACTOR
        if head == 0:
            nope_grad, rope_grad = key_grad[:, :NOPE], key_grad[:, NOPE : NOPE + ROPE]
        else:
            nope_grad, rope_grad = key_grad[:, ROPE : ROPE + NOPE], key_grad[:, ROPE + NOPE :]
        rope_grads.append(rope_grad)
        kv_grads += [nope_grad.astype(low), value_grad.astype(low)]
    kv_grad = jnp.concatenate(kv_grads, axis=1)
    rope_ref[...] += (rope_grads[0] + rope_grads[1]).reshape(rope_ref.shape)
    part = mm(turned_ref[...].reshape(LATENT, WINDOW), kv_grad, NN).astype(low)
    kept_ref[...] = part[: LATENT // 2]
    given_ref[...] = part[LATENT // 2 :]
    term_ref[...] += mm(kv_grad, weight_ref[...], NT).reshape(term_ref.shape)

    @pl.when(step == pl.num_programs(0) - 1)
    def _():
        for by in range(Y):
            at = lax.rem(spot + by, Y)
            for outs, first in ((prev_terms, 0), (own_terms, Z)):
                out = outs[by]
                out[:, :, :LATENT] = term_ref[first : first + Z, at].astype(out.dtype)
                out[:, :, LATENT:] = rope_ref[first : first + Z, at].astype(out.dtype)


def attention(spot, low_keys, own_pieces, prev_pieces, weight, query, grad_out):
    def whole(shape):
        return pl.BlockSpec(shape, lambda step: (0,) * len(shape))

    def columns(count, width):
        return pl.BlockSpec((count, width), lambda step: (0, step))

    piece = (Z, ROWS, LATENT + ROPE)
    return pl.pallas_call(
        attention_kernel,
        grid=(HEADS_DEV // 2,),
        in_specs=[
            pl.BlockSpec(memory_space=pltpu.SMEM),
            whole((1, TOK_CTX)),
            *[whole(piece)] * (2 * Y),
            columns(LATENT, 2 * KV_WIDTH),
            pl.BlockSpec(memory_space=pltpu.HBM),
            pl.BlockSpec(memory_space=pltpu.HBM),
        ],
        out_specs=[
            columns(TOK_CTX, 2 * (NOPE + ROPE)),
            columns(LATENT // 2, 2 * KV_WIDTH),
            columns(LATENT // 2, 2 * KV_WIDTH),
            *[whole(piece)] * (2 * Y),
        ],
        out_shape=[
            jax.ShapeDtypeStruct((TOK_CTX, HEADS_DEV * (NOPE + ROPE)), jnp.bfloat16),
            jax.ShapeDtypeStruct((LATENT // 2, HEADS_DEV * KV_WIDTH), jnp.bfloat16),
            jax.ShapeDtypeStruct((LATENT // 2, HEADS_DEV * KV_WIDTH), jnp.bfloat16),
            *[jax.ShapeDtypeStruct(piece, jnp.float32 if by == 0 else jnp.bfloat16) for by in range(Y)] * 2,
        ],
        scratch_shapes=[
            pltpu.VMEM((2 * Z, Y, ROWS, LATENT + ROPE), jnp.bfloat16),
            pltpu.VMEM((TOK_CTX // QUERIES, KEYS, QUERIES), jnp.float32),
            pltpu.VMEM((2 * N_CTX, PART, WINDOW), jnp.bfloat16),
            pltpu.VMEM((2 * N_CTX, PART, WINDOW), jnp.bfloat16),
            pltpu.VMEM((2 * Z, Y, ROWS, LATENT), jnp.float32),
            pltpu.VMEM((2 * Z, Y, ROWS, ROPE), jnp.float32),
            pltpu.VMEM((HEADS_DEV // 2, TOK_CTX, 2 * (NOPE + ROPE)), jnp.bfloat16),
            pltpu.VMEM((HEADS_DEV // 2, TOK_CTX, 2 * VDIM), jnp.bfloat16),
            pltpu.SemaphoreType.DMA((4,)),
        ],
        compiler_params=pltpu.CompilerParams(vmem_limit_bytes=48 * 1024 * 1024),
        cost_estimate=pl.CostEstimate(
            flops=8_000_000_000, bytes_accessed=10_000_000, transcendentals=1_600_000
        ),
        name="attention",
    )(
        spot,
        low_keys,
        *own_pieces,
        *prev_pieces,
        pltpu.with_memory_space_constraint(weight, pltpu.HBM),
        pltpu.with_memory_space_constraint(query, pltpu.HBM),
        pltpu.with_memory_space_constraint(grad_out, pltpu.HBM),
    )


def first_keys(lengths):
    starts = jnp.cumsum(lengths) - lengths
    base = lax.axis_index("ctx") * TOK_CTX
    positions = base + jnp.arange(TOK_CTX, dtype=jnp.int32)
    reached = jnp.where(starts[:, None] <= positions[None, :], starts[:, None], 0)
    return jnp.max(reached, axis=0, keepdims=True) - (base - DOC_MAX)


def summed_over_y(terms):
    total = terms[0]
    for by in range(1, Y):
        total = total + turned(terms[by], "head", by).astype(jnp.float32)
    return total


def on_device(query, kv_latent, kv_weight, grad_out, doc_lengths):
    along_z = [[z * Y + y for z in range(Z)] for y in range(Y)]
    block = jnp.broadcast_to(kv_latent, (Z, ROWS, LATENT + ROPE))
    block = lax.all_to_all(block, "head", 0, 0, axis_index_groups=along_z)
    prev_block = passed_along(block, 1)
    own_pieces = [block] + [turned(block, "head", by) for by in range(1, Y)]
    prev_pieces = [prev_block] + [turned(prev_block, "head", by) for by in range(1, Y)]
    spot = jnp.stack(
        [lax.axis_index("dp"), lax.axis_index("ctx"), lax.axis_index("head") % Y]
    ).astype(jnp.int32)
    d_query, kept, given, *terms = attention(
        spot,
        first_keys(doc_lengths[0]),
        own_pieces,
        prev_pieces,
        kv_weight,
        query[0],
        grad_out[0],
    )
    prev_term = summed_over_y(terms[Y:]).astype(jnp.bfloat16)
    term = summed_over_y(terms[:Y]) + passed_along(prev_term, -1).astype(jnp.float32)
    term = term.astype(jnp.bfloat16)
    parts = summed_weight(kept, given, prev_term, term)
    shares = lax.all_to_all(term, "head", 0, 0, axis_index_groups=along_z)
    d_latent = jnp.sum(shares.astype(jnp.float32), axis=0).astype(jnp.bfloat16)
    stacked = jax.ShapeDtypeStruct((N_CTX, *parts[0].shape), jnp.bfloat16)
    parts = small_call(stack_kernel, stacked, "stacked", *parts, after=d_latent)
    d_kv_weight = placed(parts, lax.ppermute(parts, "dp", [(0, 1), (1, 0)]))
    return (d_query[None], d_latent[None], d_kv_weight)


def solution(mesh):
    return jax.shard_map(
        on_device,
        mesh=mesh,
        in_specs=(
            P("dp", "ctx", "head"),
            P("dp", ("ctx", "head"), None),
            P(None, "head"),
            P("dp", "ctx", "head"),
            P("dp", None),
        ),
        out_specs=(P("dp", "ctx", "head"), P("dp", ("ctx", "head"), None), P(None, "head")),
        check_vma=False,
    )
```

```python
import jax
import jax.numpy as jnp
from jax import lax
from jax.experimental import pallas as pl
from jax.experimental.pallas import tpu as pltpu
from jax.sharding import PartitionSpec as P

LATENT = 512
ROPE = 64
NOPE = 128
VDIM = 128
HEADS_DEV = 4
TOK_CTX = 512
DOC_MAX = 512
QUERIES = 256
AHEAD = 1
BEHIND = 1
KEYS = QUERIES + DOC_MAX
WINDOW = TOK_CTX + DOC_MAX
KV_WIDTH = NOPE + VDIM
FACTOR = (NOPE + ROPE) ** -0.5
LOG2E = 1.4426950408889634
N_CTX = 4
Y = 4
Z = 8
ROWS = 16
PART = LATENT // 8


def passed_along(array, by):
    pairs = [(i, i + by) for i in range(N_CTX) if 0 <= i + by < N_CTX]
    return lax.ppermute(array, "ctx", pairs)


def turned(array, axis, by):
    if axis == "ctx":
        return lax.ppermute(array, axis, [(i, (i + by) % N_CTX) for i in range(N_CTX)])
    pairs = [(i, i // Y * Y + (i + by) % Y) for i in range(Z * Y)]
    return lax.ppermute(array, axis, pairs)


def first_sum_kernel(kept_ref, other_ref, after_ref, mine_ref, *out_refs):
    for by, out in enumerate([mine_ref, *out_refs]):
        at = slice(by * PART, (by + 1) * PART)
        total = kept_ref[at].astype(jnp.float32) + other_ref[at].astype(jnp.float32)
        out[...] = total.astype(out.dtype)


def second_sum_kernel(mine_ref, one_ref, two_ref, three_ref, after_ref, out_ref):
    total = mine_ref[...]
    for ref in (one_ref, two_ref, three_ref):
        total = total + ref[...].astype(jnp.float32)
    out_ref[...] = total.astype(out_ref.dtype)


def stack_kernel(one_ref, two_ref, three_ref, four_ref, after_ref, out_ref):
    for by, ref in enumerate((one_ref, two_ref, three_ref, four_ref)):
        out_ref[by] = ref[...]


def small_call(kernel, out_shape, name, *operands, after):
    vmem = pl.BlockSpec(memory_space=pltpu.VMEM)
    return pl.pallas_call(
        kernel,
        in_specs=[vmem] * len(operands) + [pl.BlockSpec(memory_space=pl.ANY)],
        out_specs=jax.tree.map(lambda _: vmem, out_shape),
        out_shape=out_shape,
        compiler_params=pltpu.CompilerParams(vmem_limit_bytes=16 * 1024 * 1024),
        name=name,
    )(*operands, after)


def summed_weight(kept, given, first_after, second_after):
    swap = [(0, 1), (1, 0)]
    other = lax.ppermute(given, "dp", swap)
    shape = (PART, given.shape[1])
    full = jax.ShapeDtypeStruct(shape, jnp.float32)
    low = jax.ShapeDtypeStruct(shape, jnp.bfloat16)
    mine, *rest = small_call(
        first_sum_kernel, [full, low, low, low], "first_sum", kept, other, after=first_after
    )
    rest = [turned(part, "ctx", by + 1) for by, part in enumerate(rest)]
    total = small_call(second_sum_kernel, low, "second_sum", mine, *rest, after=second_after)
    pieces = [total] + [turned(total, "ctx", by) for by in range(1, N_CTX)]
    return pieces


def place_kernel(core_ref, place_ref, mine_ref, other_ref, out_ref):
    core, place = core_ref[0], place_ref[0]
    for by in range(N_CTX):
        at = lax.rem(place - by + N_CTX, N_CTX)
        out_ref[core * N_CTX + at] = mine_ref[by].astype(jnp.float32)
        out_ref[(1 - core) * N_CTX + at] = other_ref[by].astype(jnp.float32)


def place_of(axis):
    return lax.axis_index(axis).astype(jnp.int32).reshape(1)


def placed(mine, other):
    vmem = pl.BlockSpec(memory_space=pltpu.VMEM)
    smem = pl.BlockSpec(memory_space=pltpu.SMEM)
    whole = pl.pallas_call(
        place_kernel,
        in_specs=[smem, smem, vmem, vmem],
        out_specs=vmem,
        out_shape=jax.ShapeDtypeStruct((2 * N_CTX, *mine.shape[1:]), jnp.float32),
        compiler_params=pltpu.CompilerParams(vmem_limit_bytes=16 * 1024 * 1024),
        name="placed",
    )(place_of("dp"), place_of("ctx"), mine, other)
    return whole.reshape(LATENT, -1)


NT = (((1,), (1,)), ((), ()))
NN = (((1,), (0,)), ((), ()))
TN = (((0,), (0,)), ((), ()))


def mm(left, right, dims):
    return lax.dot_general(left, right, dims, preferred_element_type=jnp.float32)


def attention_kernel(spot_ref, low_ref, *refs):
    own_pieces, prev_pieces, refs = refs[:Y], refs[Y : 2 * Y], refs[2 * Y :]
    weight_in, query_in, grad_in, d_query_ref, kept_ref, given_ref, *refs = refs
    own_terms, prev_terms, refs = refs[:Y], refs[Y : 2 * Y], refs[2 * Y :]
    rows_ref, plain_ref, turned_ref, term_ref, rope_ref, *refs = refs
    weight_ref, query_ref, grad_ref, copied = refs
    low = jnp.bfloat16
    core, place, spot = spot_ref[0], spot_ref[1], spot_ref[2]
    copies = [
        pltpu.make_async_copy(source, target, copied.at[at])
        for at, (source, target) in enumerate(
            ((weight_in, weight_ref), (query_in, query_ref), (grad_in, grad_ref))
        )
    ]
    for copy in copies:
        copy.start()

    for by in range(Y):
        at = lax.rem(spot - by + Y, Y)
        rows_ref[:Z, at] = prev_pieces[by][...]
        rows_ref[Z:, at] = own_pieces[by][...]
    rows = rows_ref[...].reshape(WINDOW, LATENT + ROPE)
    latent = rows[:, :LATENT]
    key_rope = rows[:, LATENT:]
    blank = jnp.zeros((WINDOW, ROPE), low)
    biases = []
    for first in range(0, TOK_CTX, QUERIES):
        key = first + lax.broadcasted_iota(jnp.int32, (KEYS, QUERIES), 0)
        query = first + DOC_MAX + lax.broadcasted_iota(jnp.int32, (KEYS, QUERIES), 1)
        start = low_ref[:, first : first + QUERIES]
        biases.append(jnp.where((key >= start) & (key <= query), 0.0, -1e30))
    for copy in copies:
        copy.wait()

    kv_rows = mm(latent, weight_ref[...], NN).astype(low)
    keys, values = [], []
    for head in range(HEADS_DEV):
        key_nope = kv_rows[:, head * KV_WIDTH : head * KV_WIDTH + NOPE]
        parts = [key_nope, key_rope, blank] if head % 2 == 0 else [blank, key_nope, key_rope]
        keys.append(jnp.concatenate(parts, axis=1))
        values.append(kv_rows[:, head * KV_WIDTH + NOPE : (head + 1) * KV_WIDTH])
    spans = [(head, first) for head in range(HEADS_DEV) for first in range(0, TOK_CTX, QUERIES)]

    def operands(head, first):
        rows_at = slice(first, first + QUERIES)
        left = head // 2 * 2 * (NOPE + ROPE) + head % 2 * NOPE
        queries = query_ref[rows_at, left : left + 2 * NOPE]
        return queries, grad_ref[rows_at, head * VDIM : (head + 1) * VDIM]

    def products(head, first):
        queries, upstream = operands(head, first)
        scores = mm(keys[head][first : first + KEYS], queries, NT)
        return scores, mm(values[head][first : first + KEYS], upstream, NT)

    def slopes(first, scores, dots):
        scores = scores * (FACTOR * LOG2E) + biases[first // QUERIES]
        weights = jnp.exp2(scores - jnp.max(scores, axis=0, keepdims=True))
        prob = weights * (1.0 / jnp.sum(weights, axis=0, keepdims=True))
        prob_low = prob.astype(low)
        delta = jnp.sum(prob_low.astype(jnp.float32) * dots, axis=0, keepdims=True)
        return prob_low, (prob * (dots - delta)).astype(low)

    def gradients(head, first, prob_low, slope):
        queries, upstream = operands(head, first)
        d_query = mm(slope, keys[head][first : first + KEYS], TN) * FACTOR
        at = slice(first, first + QUERIES)
        left = head // 2 * 2 * (NOPE + ROPE)
        if head % 2 == 0:
            d_query_ref[at, left : left + NOPE] = d_query[:, :NOPE].astype(low)
            middle[first] = d_query[:, NOPE:]
        else:
            whole = middle[first] + d_query[:, :NOPE]
            d_query_ref[at, left + NOPE : left + 2 * NOPE] = whole.astype(low)
            d_query_ref[at, left + 2 * NOPE : left + 3 * NOPE] = d_query[:, NOPE:].astype(low)
        return mm(slope, queries, NN), mm(prob_low, upstream, NN)

    middle, grads = {}, []
    made, held = {}, {}
    count = len(spans)
    for turn in range(-AHEAD, count + BEHIND):
        if turn + AHEAD < count:
            made[turn + AHEAD] = products(*spans[turn + AHEAD])
        if 0 <= turn < count:
            held[turn] = slopes(spans[turn][1], *made.pop(turn))
        if 0 <= turn - BEHIND:
            grads.append(gradients(*spans[turn - BEHIND], *held.pop(turn - BEHIND)))

    kv_grads, rope_grads = [], []
    for head in range(HEADS_DEV):
        key_grad, value_grad = (
            jnp.concatenate(
                [one[:QUERIES], one[QUERIES:] + two[:-QUERIES], two[-QUERIES:]], axis=0
            )
            for one, two in zip(*grads[2 * head : 2 * head + 2])
        )
        key_grad = key_grad * FACTOR
        if head % 2 == 0:
            nope_grad, rope_grad = key_grad[:, :NOPE], key_grad[:, NOPE : NOPE + ROPE]
        else:
            nope_grad, rope_grad = key_grad[:, ROPE : ROPE + NOPE], key_grad[:, ROPE + NOPE :]
        rope_grads.append(rope_grad)
        kv_grads += [nope_grad.astype(low), value_grad.astype(low)]
    kv_grad = jnp.concatenate(kv_grads, axis=1)
    rope_ref[...] = sum(rope_grads[1:], rope_grads[0]).reshape(rope_ref.shape)
    term_ref[...] = mm(kv_grad, weight_ref[...], NT).reshape(term_ref.shape)
    plain_ref[...] = latent.T.reshape(2 * N_CTX, PART, WINDOW)
    for by in range(N_CTX):
        at = lax.rem(place + by, N_CTX)
        turned_ref[by] = plain_ref[core * N_CTX + at]
        turned_ref[N_CTX + by] = plain_ref[(1 - core) * N_CTX + at]
    part = mm(turned_ref[...].reshape(LATENT, WINDOW), kv_grad, NN).astype(low)
    kept_ref[...] = part[: LATENT // 2]
    given_ref[...] = part[LATENT // 2 :]

    for by in range(Y):
        at = lax.rem(spot + by, Y)
        for outs, first in ((prev_terms, 0), (own_terms, Z)):
            out = outs[by]
            out[:, :, :LATENT] = term_ref[first : first + Z, at].astype(out.dtype)
            out[:, :, LATENT:] = rope_ref[first : first + Z, at].astype(out.dtype)


def attention(spot, low_keys, own_pieces, prev_pieces, weight, query, grad_out):
    vmem = pl.BlockSpec(memory_space=pltpu.VMEM)
    hbm = pl.BlockSpec(memory_space=pltpu.HBM)
    piece = (Z, ROWS, LATENT + ROPE)
    return pl.pallas_call(
        attention_kernel,
        in_specs=[
            pl.BlockSpec(memory_space=pltpu.SMEM),
            vmem,
            *[vmem] * (2 * Y),
            hbm,
            hbm,
            hbm,
        ],
        out_specs=[vmem] * (3 + 2 * Y),
        out_shape=[
            jax.ShapeDtypeStruct((TOK_CTX, HEADS_DEV * (NOPE + ROPE)), jnp.bfloat16),
            jax.ShapeDtypeStruct((LATENT // 2, HEADS_DEV * KV_WIDTH), jnp.bfloat16),
            jax.ShapeDtypeStruct((LATENT // 2, HEADS_DEV * KV_WIDTH), jnp.bfloat16),
            *[jax.ShapeDtypeStruct(piece, jnp.float32 if by == 0 else jnp.bfloat16) for by in range(Y)] * 2,
        ],
        scratch_shapes=[
            pltpu.VMEM((2 * Z, Y, ROWS, LATENT + ROPE), jnp.bfloat16),
            pltpu.VMEM((2 * N_CTX, PART, WINDOW), jnp.bfloat16),
            pltpu.VMEM((2 * N_CTX, PART, WINDOW), jnp.bfloat16),
            pltpu.VMEM((2 * Z, Y, ROWS, LATENT), jnp.float32),
            pltpu.VMEM((2 * Z, Y, ROWS, ROPE), jnp.float32),
            pltpu.VMEM((LATENT, HEADS_DEV * KV_WIDTH), jnp.bfloat16),
            pltpu.VMEM((TOK_CTX, HEADS_DEV * (NOPE + ROPE)), jnp.bfloat16),
            pltpu.VMEM((TOK_CTX, HEADS_DEV * VDIM), jnp.bfloat16),
            pltpu.SemaphoreType.DMA((3,)),
        ],
        compiler_params=pltpu.CompilerParams(vmem_limit_bytes=48 * 1024 * 1024),
        cost_estimate=pl.CostEstimate(
            flops=8_000_000_000, bytes_accessed=10_000_000, transcendentals=1_600_000
        ),
        name="attention",
    )(
        spot,
        low_keys,
        *own_pieces,
        *prev_pieces,
        pltpu.with_memory_space_constraint(weight, pltpu.HBM),
        pltpu.with_memory_space_constraint(query, pltpu.HBM),
        pltpu.with_memory_space_constraint(grad_out, pltpu.HBM),
    )


def first_keys(lengths):
    starts = jnp.cumsum(lengths) - lengths
    base = lax.axis_index("ctx") * TOK_CTX
    positions = base + jnp.arange(TOK_CTX, dtype=jnp.int32)
    reached = jnp.where(starts[:, None] <= positions[None, :], starts[:, None], 0)
    return jnp.max(reached, axis=0, keepdims=True) - (base - DOC_MAX)


def summed_over_y(terms):
    total = terms[0]
    for by in range(1, Y):
        total = total + turned(terms[by], "head", by).astype(jnp.float32)
    return total


def on_device(query, kv_latent, kv_weight, grad_out, doc_lengths):
    along_z = [[z * Y + y for z in range(Z)] for y in range(Y)]
    block = jnp.broadcast_to(kv_latent, (Z, ROWS, LATENT + ROPE))
    block = lax.all_to_all(block, "head", 0, 0, axis_index_groups=along_z)
    prev_block = passed_along(block, 1)
    own_pieces = [block] + [turned(block, "head", by) for by in range(1, Y)]
    prev_pieces = [prev_block] + [turned(prev_block, "head", by) for by in range(1, Y)]
    spot = jnp.stack(
        [lax.axis_index("dp"), lax.axis_index("ctx"), lax.axis_index("head") % Y]
    ).astype(jnp.int32)
    d_query, kept, given, *terms = attention(
        spot,
        first_keys(doc_lengths[0]),
        own_pieces,
        prev_pieces,
        kv_weight,
        query[0],
        grad_out[0],
    )
    prev_term = summed_over_y(terms[Y:]).astype(jnp.bfloat16)
    term = summed_over_y(terms[:Y]) + passed_along(prev_term, -1).astype(jnp.float32)
    term = term.astype(jnp.bfloat16)
    parts = summed_weight(kept, given, prev_term, term)
    shares = lax.all_to_all(term, "head", 0, 0, axis_index_groups=along_z)
    d_latent = jnp.sum(shares.astype(jnp.float32), axis=0).astype(jnp.bfloat16)
    stacked = jax.ShapeDtypeStruct((N_CTX, *parts[0].shape), jnp.bfloat16)
    parts = small_call(stack_kernel, stacked, "stacked", *parts, after=d_latent)
    d_kv_weight = placed(parts, lax.ppermute(parts, "dp", [(0, 1), (1, 0)]))
    return (d_query[None], d_latent[None], d_kv_weight)


def solution(mesh):
    return jax.shard_map(
        on_device,
        mesh=mesh,
        in_specs=(
            P("dp", "ctx", "head"),
            P("dp", ("ctx", "head"), None),
            P(None, "head"),
            P("dp", "ctx", "head"),
            P("dp", None),
        ),
        out_specs=(P("dp", "ctx", "head"), P("dp", ("ctx", "head"), None), P(None, "head")),
        check_vma=False,
    )
```

```python
import jax
import jax.numpy as jnp
from jax import lax
from jax.experimental import pallas as pl
from jax.experimental.pallas import tpu as pltpu
from jax.sharding import PartitionSpec as P

LATENT = 512
ROPE = 64
NOPE = 128
VDIM = 128
HEADS_DEV = 4
TOK_CTX = 512
DOC_MAX = 512
QUERIES = 256
AHEAD = 1
BEHIND = 1
KEYS = QUERIES + DOC_MAX
WINDOW = TOK_CTX + DOC_MAX
KV_WIDTH = NOPE + VDIM
FACTOR = (NOPE + ROPE) ** -0.5
LOG2E = 1.4426950408889634
N_CTX = 4
Y = 4
Z = 8
ROWS = 16
PART = LATENT // 8


def passed_along(array, by):
    pairs = [(i, i + by) for i in range(N_CTX) if 0 <= i + by < N_CTX]
    return lax.ppermute(array, "ctx", pairs)


def turned(array, axis, by):
    if axis == "ctx":
        return lax.ppermute(array, axis, [(i, (i + by) % N_CTX) for i in range(N_CTX)])
    pairs = [(i, i // Y * Y + (i + by) % Y) for i in range(Z * Y)]
    return lax.ppermute(array, axis, pairs)


def first_sum_kernel(kept_ref, other_ref, after_ref, mine_ref, *out_refs):
    for by, out in enumerate([mine_ref, *out_refs]):
        at = slice(by * PART, (by + 1) * PART)
        total = kept_ref[at].astype(jnp.float32) + other_ref[at].astype(jnp.float32)
        out[...] = total.astype(out.dtype)


def second_sum_kernel(mine_ref, one_ref, two_ref, three_ref, after_ref, out_ref):
    total = mine_ref[...]
    for ref in (one_ref, two_ref, three_ref):
        total = total + ref[...].astype(jnp.float32)
    out_ref[...] = total.astype(out_ref.dtype)


def stack_kernel(one_ref, two_ref, three_ref, four_ref, after_ref, out_ref):
    for by, ref in enumerate((one_ref, two_ref, three_ref, four_ref)):
        out_ref[by] = ref[...]


def small_call(kernel, out_shape, name, *operands, after):
    vmem = pl.BlockSpec(memory_space=pltpu.VMEM)
    return pl.pallas_call(
        kernel,
        in_specs=[vmem] * len(operands) + [pl.BlockSpec(memory_space=pl.ANY)],
        out_specs=jax.tree.map(lambda _: vmem, out_shape),
        out_shape=out_shape,
        compiler_params=pltpu.CompilerParams(vmem_limit_bytes=16 * 1024 * 1024),
        name=name,
    )(*operands, after)


def summed_weight(kept, given, first_after, second_after):
    swap = [(0, 1), (1, 0)]
    other = lax.ppermute(given, "dp", swap)
    shape = (PART, given.shape[1])
    full = jax.ShapeDtypeStruct(shape, jnp.float32)
    low = jax.ShapeDtypeStruct(shape, jnp.bfloat16)
    mine, *rest = small_call(
        first_sum_kernel, [full, low, low, low], "first_sum", kept, other, after=first_after
    )
    rest = [turned(part, "ctx", by + 1) for by, part in enumerate(rest)]
    total = small_call(second_sum_kernel, low, "second_sum", mine, *rest, after=second_after)
    pieces = [total] + [turned(total, "ctx", by) for by in range(1, N_CTX)]
    return pieces


def place_kernel(core_ref, place_ref, given_ref, *refs):
    for by in range(N_CTX):
        at = lax.rem(place_ref[0] - by + N_CTX, N_CTX)
        refs[-1][at] = given_ref[by].astype(jnp.float32)


def place_of(axis):
    return lax.axis_index(axis).astype(jnp.int32).reshape(1)


def placed(given, half, whole, name):
    shape = given.shape
    first = whole is None
    return pl.pallas_call(
        place_kernel,
        grid_spec=pltpu.PrefetchScalarGridSpec(
            num_scalar_prefetch=2,
            grid=(1,),
            in_specs=[pl.BlockSpec(shape, lambda step, half, place: (0, 0, 0))]
            + [pl.BlockSpec(memory_space=pl.ANY)] * (not first),
            out_specs=pl.BlockSpec(shape, lambda step, half, place: (half[0], 0, 0)),
        ),
        out_shape=jax.ShapeDtypeStruct((2 * N_CTX, *shape[1:]), jnp.float32),
        input_output_aliases={} if first else {3: 0},
        compiler_params=pltpu.CompilerParams(vmem_limit_bytes=16 * 1024 * 1024),
        name=name,
    )(half, place_of("ctx"), given, *([] if first else [whole]))


NT = (((1,), (1,)), ((), ()))
NN = (((1,), (0,)), ((), ()))
TN = (((0,), (0,)), ((), ()))


def mm(left, right, dims):
    return lax.dot_general(left, right, dims, preferred_element_type=jnp.float32)


def attention_kernel(spot_ref, low_ref, *refs):
    own_pieces, prev_pieces, refs = refs[:Y], refs[Y : 2 * Y], refs[2 * Y :]
    weight_in, query_in, grad_in, d_query_ref, kept_ref, given_ref, *refs = refs
    own_terms, prev_terms, refs = refs[:Y], refs[Y : 2 * Y], refs[2 * Y :]
    rows_ref, plain_ref, turned_ref, term_ref, rope_ref, *refs = refs
    weight_ref, query_ref, grad_ref, copied = refs
    low = jnp.bfloat16
    core, place, spot = spot_ref[0], spot_ref[1], spot_ref[2]
    copies = [
        pltpu.make_async_copy(source, target, copied.at[at])
        for at, (source, target) in enumerate(
            ((weight_in, weight_ref), (query_in, query_ref), (grad_in, grad_ref))
        )
    ]
    for copy in copies:
        copy.start()

    for by in range(Y):
        at = lax.rem(spot - by + Y, Y)
        rows_ref[:Z, at] = prev_pieces[by][...]
        rows_ref[Z:, at] = own_pieces[by][...]
    rows = rows_ref[...].reshape(WINDOW, LATENT + ROPE)
    latent = rows[:, :LATENT]
    key_rope = rows[:, LATENT:]
    blank = jnp.zeros((WINDOW, ROPE), low)
    biases = []
    for first in range(0, TOK_CTX, QUERIES):
        key = first + lax.broadcasted_iota(jnp.int32, (KEYS, QUERIES), 0)
        query = first + DOC_MAX + lax.broadcasted_iota(jnp.int32, (KEYS, QUERIES), 1)
        start = low_ref[:, first : first + QUERIES]
        biases.append(jnp.where((key >= start) & (key <= query), 0.0, -1e30))
    for copy in copies:
        copy.wait()

    kv_rows = mm(latent, weight_ref[...], NN).astype(low)
    keys, values = [], []
    for head in range(HEADS_DEV):
        key_nope = kv_rows[:, head * KV_WIDTH : head * KV_WIDTH + NOPE]
        parts = [key_nope, key_rope, blank] if head % 2 == 0 else [blank, key_nope, key_rope]
        keys.append(jnp.concatenate(parts, axis=1))
        values.append(kv_rows[:, head * KV_WIDTH + NOPE : (head + 1) * KV_WIDTH])
    spans = [(head, first) for head in range(HEADS_DEV) for first in range(0, TOK_CTX, QUERIES)]

    def operands(head, first):
        rows_at = slice(first, first + QUERIES)
        left = head // 2 * 2 * (NOPE + ROPE) + head % 2 * NOPE
        queries = query_ref[rows_at, left : left + 2 * NOPE]
        return queries, grad_ref[rows_at, head * VDIM : (head + 1) * VDIM]

    def products(head, first):
        queries, upstream = operands(head, first)
        scores = mm(keys[head][first : first + KEYS], queries, NT)
        return scores, mm(values[head][first : first + KEYS], upstream, NT)

    def slopes(first, scores, dots):
        scores = scores * (FACTOR * LOG2E) + biases[first // QUERIES]
        weights = jnp.exp2(scores - jnp.max(scores, axis=0, keepdims=True))
        prob = weights * (1.0 / jnp.sum(weights, axis=0, keepdims=True))
        prob_low = prob.astype(low)
        delta = jnp.sum(prob_low.astype(jnp.float32) * dots, axis=0, keepdims=True)
        return prob_low, (prob * (dots - delta)).astype(low)

    def gradients(head, first, prob_low, slope):
        queries, upstream = operands(head, first)
        d_query = mm(slope, keys[head][first : first + KEYS], TN) * FACTOR
        at = slice(first, first + QUERIES)
        left = head // 2 * 2 * (NOPE + ROPE)
        if head % 2 == 0:
            d_query_ref[at, left : left + NOPE] = d_query[:, :NOPE].astype(low)
            middle[first] = d_query[:, NOPE:]
        else:
            whole = middle[first] + d_query[:, :NOPE]
            d_query_ref[at, left + NOPE : left + 2 * NOPE] = whole.astype(low)
            d_query_ref[at, left + 2 * NOPE : left + 3 * NOPE] = d_query[:, NOPE:].astype(low)
        return mm(slope, queries, NN), mm(prob_low, upstream, NN)

    middle, grads = {}, []
    made, held = {}, {}
    count = len(spans)
    for turn in range(-AHEAD, count + BEHIND):
        if turn + AHEAD < count:
            made[turn + AHEAD] = products(*spans[turn + AHEAD])
        if 0 <= turn < count:
            held[turn] = slopes(spans[turn][1], *made.pop(turn))
        if 0 <= turn - BEHIND:
            grads.append(gradients(*spans[turn - BEHIND], *held.pop(turn - BEHIND)))

    kv_grads, rope_grads = [], []
    for head in range(HEADS_DEV):
        key_grad, value_grad = (
            jnp.concatenate(
                [one[:QUERIES], one[QUERIES:] + two[:-QUERIES], two[-QUERIES:]], axis=0
            )
            for one, two in zip(*grads[2 * head : 2 * head + 2])
        )
        key_grad = key_grad * FACTOR
        if head % 2 == 0:
            nope_grad, rope_grad = key_grad[:, :NOPE], key_grad[:, NOPE : NOPE + ROPE]
        else:
            nope_grad, rope_grad = key_grad[:, ROPE : ROPE + NOPE], key_grad[:, ROPE + NOPE :]
        rope_grads.append(rope_grad)
        kv_grads += [nope_grad.astype(low), value_grad.astype(low)]
    kv_grad = jnp.concatenate(kv_grads, axis=1)
    rope_ref[...] = sum(rope_grads[1:], rope_grads[0]).reshape(rope_ref.shape)
    term_ref[...] = mm(kv_grad, weight_ref[...], NT).reshape(term_ref.shape)
    plain_ref[...] = latent.T.reshape(2 * N_CTX, PART, WINDOW)
    for by in range(N_CTX):
        at = lax.rem(place + by, N_CTX)
        turned_ref[by] = plain_ref[core * N_CTX + at]
        turned_ref[N_CTX + by] = plain_ref[(1 - core) * N_CTX + at]
    part = mm(turned_ref[...].reshape(LATENT, WINDOW), kv_grad, NN).astype(low)
    kept_ref[...] = part[: LATENT // 2]
    given_ref[...] = part[LATENT // 2 :]

    for by in range(Y):
        at = lax.rem(spot + by, Y)
        for outs, first in ((prev_terms, 0), (own_terms, Z)):
            out = outs[by]
            out[:, :, :LATENT] = term_ref[first : first + Z, at].astype(out.dtype)
            out[:, :, LATENT:] = rope_ref[first : first + Z, at].astype(out.dtype)


def attention(spot, low_keys, own_pieces, prev_pieces, weight, query, grad_out):
    vmem = pl.BlockSpec(memory_space=pltpu.VMEM)
    hbm = pl.BlockSpec(memory_space=pltpu.HBM)
    piece = (Z, ROWS, LATENT + ROPE)
    return pl.pallas_call(
        attention_kernel,
        in_specs=[
            pl.BlockSpec(memory_space=pltpu.SMEM),
            vmem,
            *[vmem] * (2 * Y),
            hbm,
            hbm,
            hbm,
        ],
        out_specs=[vmem] * (3 + 2 * Y),
        out_shape=[
            jax.ShapeDtypeStruct((TOK_CTX, HEADS_DEV * (NOPE + ROPE)), jnp.bfloat16),
            jax.ShapeDtypeStruct((LATENT // 2, HEADS_DEV * KV_WIDTH), jnp.bfloat16),
            jax.ShapeDtypeStruct((LATENT // 2, HEADS_DEV * KV_WIDTH), jnp.bfloat16),
            *[jax.ShapeDtypeStruct(piece, jnp.float32 if by == 0 else jnp.bfloat16) for by in range(Y)] * 2,
        ],
        scratch_shapes=[
            pltpu.VMEM((2 * Z, Y, ROWS, LATENT + ROPE), jnp.bfloat16),
            pltpu.VMEM((2 * N_CTX, PART, WINDOW), jnp.bfloat16),
            pltpu.VMEM((2 * N_CTX, PART, WINDOW), jnp.bfloat16),
            pltpu.VMEM((2 * Z, Y, ROWS, LATENT), jnp.float32),
            pltpu.VMEM((2 * Z, Y, ROWS, ROPE), jnp.float32),
            pltpu.VMEM((LATENT, HEADS_DEV * KV_WIDTH), jnp.bfloat16),
            pltpu.VMEM((TOK_CTX, HEADS_DEV * (NOPE + ROPE)), jnp.bfloat16),
            pltpu.VMEM((TOK_CTX, HEADS_DEV * VDIM), jnp.bfloat16),
            pltpu.SemaphoreType.DMA((3,)),
        ],
        compiler_params=pltpu.CompilerParams(vmem_limit_bytes=48 * 1024 * 1024),
        cost_estimate=pl.CostEstimate(
            flops=8_000_000_000, bytes_accessed=10_000_000, transcendentals=1_600_000
        ),
        name="attention",
    )(
        spot,
        low_keys,
        *own_pieces,
        *prev_pieces,
        pltpu.with_memory_space_constraint(weight, pltpu.HBM),
        pltpu.with_memory_space_constraint(query, pltpu.HBM),
        pltpu.with_memory_space_constraint(grad_out, pltpu.HBM),
    )


def first_keys(lengths):
    starts = jnp.cumsum(lengths) - lengths
    base = lax.axis_index("ctx") * TOK_CTX
    positions = base + jnp.arange(TOK_CTX, dtype=jnp.int32)
    reached = jnp.where(starts[:, None] <= positions[None, :], starts[:, None], 0)
    return jnp.max(reached, axis=0, keepdims=True) - (base - DOC_MAX)


def summed_over_y(terms):
    total = terms[0]
    for by in range(1, Y):
        total = total + turned(terms[by], "head", by).astype(jnp.float32)
    return total


def on_device(query, kv_latent, kv_weight, grad_out, doc_lengths):
    along_z = [[z * Y + y for z in range(Z)] for y in range(Y)]
    block = jnp.broadcast_to(kv_latent, (Z, ROWS, LATENT + ROPE))
    block = lax.all_to_all(block, "head", 0, 0, axis_index_groups=along_z)
    prev_block = passed_along(block, 1)
    own_pieces = [block] + [turned(block, "head", by) for by in range(1, Y)]
    prev_pieces = [prev_block] + [turned(prev_block, "head", by) for by in range(1, Y)]
    spot = jnp.stack(
        [lax.axis_index("dp"), lax.axis_index("ctx"), lax.axis_index("head") % Y]
    ).astype(jnp.int32)
    d_query, kept, given, *terms = attention(
        spot,
        first_keys(doc_lengths[0]),
        own_pieces,
        prev_pieces,
        kv_weight,
        query[0],
        grad_out[0],
    )
    prev_term = summed_over_y(terms[Y:]).astype(jnp.bfloat16)
    term = summed_over_y(terms[:Y]) + passed_along(prev_term, -1).astype(jnp.float32)
    term = term.astype(jnp.bfloat16)
    parts = summed_weight(kept, given, prev_term, term)
    shares = lax.all_to_all(term, "head", 0, 0, axis_index_groups=along_z)
    d_latent = jnp.sum(shares.astype(jnp.float32), axis=0).astype(jnp.bfloat16)
    stacked = jax.ShapeDtypeStruct((N_CTX, *parts[0].shape), jnp.bfloat16)
    parts = small_call(stack_kernel, stacked, "stacked", *parts, after=shares)
    other = lax.ppermute(parts, "dp", [(0, 1), (1, 0)])
    core = place_of("dp")
    d_kv_weight = placed(parts, core, None, "mine")
    d_kv_weight = placed(other, 1 - core, d_kv_weight, "other").reshape(LATENT, -1)
    return (d_query[None], d_latent[None], d_kv_weight)


def solution(mesh):
    return jax.shard_map(
        on_device,
        mesh=mesh,
        in_specs=(
            P("dp", "ctx", "head"),
            P("dp", ("ctx", "head"), None),
            P(None, "head"),
            P("dp", "ctx", "head"),
            P("dp", None),
        ),
        out_specs=(P("dp", "ctx", "head"), P("dp", ("ctx", "head"), None), P(None, "head")),
        check_vma=False,
    )
```
